128 devices in a mesh: gx: 8 (over y, core), gy: 16 (over z, x).
Axes of the slice: x: 4, y: 4, z: 4, core: 2. Of those that a mesh axis runs over, the one named last changes fastest.
Arguments:
- atmosphere_surface_fields: float32 [20, 2097152], P(None, ('gx', 'gy')), may hold values from -6 to 6
- ocean_surface_fields: float32 [20, 2097152], P(None, ('gx', 'gy')), may hold values from -6 to 6
- atm_area: float32 [2097152], P(('gx', 'gy')), may hold values from 1 to 4
- ocn_area: float32 [2097152], P(('gx', 'gy')), may hold values from 1 to 4
- send_atm: int32 [128, 9, 24], P(('gx', 'gy')), may hold values from -1 to 127, as said below
- send_ocn: int32 [128, 9, 24], P(('gx', 'gy')), may hold values from -1 to 127, as said below
- atm_ref: int32 [8388608], P(('gx', 'gy')), may hold values from 0 to 27647, as said below
- ocn_ref: int32 [8388608], P(('gx', 'gy')), may hold values from 0 to 27647, as said below
- cell_area: float32 [8388608], P(('gx', 'gy')), may hold values from 0.1 to 1
- cell_mask: int32 [8388608], P(('gx', 'gy')), may hold values 0 or 1
- cell_count: int32 [128], P(('gx', 'gy')), may hold values from 8192 to 65536, as said below
Outputs:
- atm_flux: float32 [18, 2097152], P(None, ('gx', 'gy'))
- ocn_flux: float32 [18, 2097152], P(None, ('gx', 'gy'))
The draws below stay inside these ranges and needn't reach their ends.
Inputs may be any that keep to these rules, and one draw needn't show every extreme that they name: `send_atm`: in each row [s, n] the first one to 24 entries are distinct blocks of device s and the rest are -1; rows [s, 4] and [s, 8] are full, and some owner receives full rows from all its neighbours. `send_ocn`: in each row [s, n] the first one to 24 entries are distinct blocks of device s and the rest are -1; rows [s, 4] and [s, 8] are full, and some owner receives full rows from all its neighbours. `atm_ref`: every cell, live or not, names a slot whose entry in send_atm is not -1; the 32 cells of each aligned group of 32 cells name the same slot. `ocn_ref`: every cell, live or not, names a slot whose entry in send_ocn is not -1; the 32 cells of each aligned group of 32 cells name the same slot. `cell_count`: some owner has all 65536 cells live.
All inputs are finite; a program needn't handle non-finite values. No bound on the sum of `cell_mask` on one device may be relied on, other than what follows from the above.
Results may differ from the reference program's by a relative error of at most 0.0003.
Values sent between devices are 32-bit elements; how exact they have to be, the bound alone decides.
No kernel may reach another device: no remote copies, remote signals or barrier semaphores. Data moves between devices by JAX's collectives and lax.ppermute only.
A program may use at most 192 MiB of HBM per device.

```python
import math
import jax
import jax.numpy as jnp
from jax import lax

F = 20
FR = 18
NB = 9
CAP = 24
GRP = 32
A_BLK_DEV = 128
O_BLK_DEV = 128
XC_DEV = 65536
ITERS = 6
OWNERS = 128
NA = 2097152
NO = 2097152
NXC = 8388608
N_GX = 8
N_GY = 16


def owner_of(source, neighbor):
    offset_x = neighbor // 3 - 1
    offset_y = neighbor % 3 - 1
    return (source // N_GY + offset_x) % N_GX * N_GY + (source % N_GY + offset_y) % N_GY


def pair_counts(key, salt):
    sub = jax.random.fold_in(key, salt)
    count_key, owner_key = jax.random.split(sub)
    counts = jax.random.randint(count_key, (OWNERS, NB), max(1, CAP // 2), CAP + 1)
    chosen = jax.random.randint(owner_key, (), 0, OWNERS)
    sources = jnp.arange(OWNERS)[:, None]
    neighbors = jnp.arange(NB)[None, :]
    full = (neighbors == 4) | (neighbors == NB - 1) | (owner_of(sources, neighbors) == chosen)
    return jnp.where(full, CAP, counts).astype(jnp.int32)


def block_lists(key, salt, blocks_dev):
    counts = pair_counts(key, salt)
    key = jax.random.fold_in(key, salt + 100)
    first_key, second_key = jax.random.split(key)
    base = jax.random.randint(first_key, (OWNERS, NB), 0, blocks_dev)
    stride = jax.random.randint(second_key, (OWNERS, NB), 1, (blocks_dev - 1) // (CAP - 1) + 1)
    steps_in = jnp.arange(CAP).astype(jnp.int32)
    picked = (base[:, :, None] + steps_in[None, None, :] * stride[:, :, None]) % blocks_dev
    return jnp.where(steps_in[None, None, :] < counts[:, :, None], picked, -1).astype(jnp.int32)


def cell_refs(key, salt):
    counts = pair_counts(key, salt)
    key = jax.random.fold_in(key, salt + 200)
    key_shift, key_slot, key_lane = jax.random.split(key, 3)
    groups_dev = XC_DEV // GRP
    ngroups = NXC // GRP
    group_owner = (jnp.arange(ngroups) // groups_dev).astype(jnp.int32)
    group_local = (jnp.arange(ngroups) % groups_dev).astype(jnp.int32)
    rotate = jax.random.randint(key_shift, (OWNERS,), 0, NB)
    neighbor = (group_local + rotate[group_owner]) % NB
    neighbor = jnp.where(group_local == 0, NB - 1, jnp.where(group_local == 1, 0, neighbor))
    offset_x = neighbor // 3 - 1
    offset_y = neighbor % 3 - 1
    source = (group_owner // N_GY - offset_x) % N_GX * N_GY + (group_owner % N_GY - offset_y) % N_GY
    within = jax.random.randint(key_slot, (ngroups,), 0, 2 ** 20) % counts[source, neighbor]
    within = jnp.where(group_local == 0, CAP - 1, jnp.where(group_local == 1, 0, within))
    slot = jnp.repeat(neighbor * CAP + within, GRP)
    local_index = (jnp.arange(NXC) % XC_DEV).astype(jnp.int32)
    lane = jax.random.randint(key_lane, (NXC,), 0, 128)
    lane = jnp.where(local_index == 0, 127, jnp.where(local_index == GRP, 0, lane))
    return (slot * 128 + lane).astype(jnp.int32)


def draw_send_atm(key, part):
    return block_lists(key, 11, A_BLK_DEV)


def draw_send_ocn(key, part):
    return block_lists(key, 12, O_BLK_DEV)


def draw_atm_ref(key, part):
    return cell_refs(key, 11)


def draw_ocn_ref(key, part):
    return cell_refs(key, 12)


def draw_cell_count(key, part):
    key = jax.random.fold_in(key, 5)
    key_div, key_perm = jax.random.split(key)
    divisor = jax.random.randint(key_div, (OWNERS,), 1, 9)
    order = jax.random.permutation(key_perm, OWNERS)
    position = jnp.arange(OWNERS)
    divisor = jnp.where(position == order[0], 1, jnp.where(position == order[1], 8, divisor))
    return (XC_DEV // divisor).astype(jnp.int32)


def place_ends(array, own_key, smallest, high):
    shape = array.shape
    place = [jax.random.randint(jax.random.fold_in(own_key, axis), (), 0, shape[axis]) for axis in range(len(shape))]
    array = array.at[tuple(place)].set(smallest)
    longest = shape.index(max(shape))
    place[longest] = (place[longest] + 1) % shape[longest]
    return array.at[tuple(place)].set(high)


def levels(key, dims, shards, smallest, top_value):
    loudness = 1.0
    for axis_at, parts in shards:
        steps = jax.random.uniform(jax.random.fold_in(jax.random.fold_in(key, 6), axis_at), (parts,), jnp.float32, smallest / len(shards), top_value / len(shards))
        loudness = loudness * jnp.repeat(jnp.exp(steps), dims[axis_at] // parts).reshape((-1,) + (1,) * (len(dims) - 1 - axis_at))
    return loudness


def bell_draw(own_key, extent, scale, limit, cuts=(), kind=jnp.bfloat16):
    drawn = scale * jax.random.normal(own_key, extent, jnp.float32)
    if cuts:
        drawn = drawn * levels(own_key, extent, cuts, -0.22, 0.18)
    return jnp.clip(drawn, -limit, limit).astype(kind)


def setup_inputs(seed: int = 0) -> dict:
    seeds = jax.random.split(jax.random.key(seed), 12)
    return {
        "atmosphere_surface_fields": bell_draw(seeds[0], (F, NA), 1.0, 6.0, ((1, 128),), jnp.float32),
        "ocean_surface_fields": bell_draw(seeds[1], (F, NO), 1.0, 6.0, ((1, 128),), jnp.float32),
        "atm_area": jnp.clip(jnp.exp(math.log(4.0) - 1.3862944 * jax.random.uniform(seeds[2], (NA,), jnp.float32) ** levels(seeds[2], (NA,), ((0, 128),), -0.2, 0.2)), 1.0, 4.0),
        "ocn_area": jnp.clip(jnp.exp(math.log(4.0) - 1.3862944 * jax.random.uniform(seeds[3], (NO,), jnp.float32) ** levels(seeds[3], (NO,), ((0, 128),), -0.2, 0.2)), 1.0, 4.0),
        "send_atm": draw_send_atm(jax.random.fold_in(seeds[11], 71), 0),
        "send_ocn": draw_send_ocn(jax.random.fold_in(seeds[11], 71), 0),
        "atm_ref": draw_atm_ref(jax.random.fold_in(seeds[11], 71), 0),
        "ocn_ref": draw_ocn_ref(jax.random.fold_in(seeds[11], 71), 0),
        "cell_area": jnp.clip(jnp.exp(math.log(1.0) - 2.3025851 * jax.random.uniform(seeds[8], (NXC,), jnp.float32) ** levels(seeds[8], (NXC,), ((0, 128),), -0.2, 0.2)), 0.1, 1.0),
        "cell_mask": place_ends((jax.random.randint(seeds[9], (NXC,), 0, 4) < 3).astype(jnp.int32), jax.random.fold_in(seeds[9], 1), 0, 1),
        "cell_count": draw_cell_count(jax.random.fold_in(seeds[11], 71), 0),
    }


KAPPA = 0.4
GRAVITY = 9.8
FLUX_SCALE = 25.0

def surface_flux(atmos, ocean):
    shear_x = 6.0 * atmos[0] - 0.3 * ocean[0]
    shear_y = 6.0 * atmos[1] - 0.3 * ocean[1]
    wind_speed = jnp.sqrt(shear_x * shear_x + shear_y * shear_y + 0.25 + 0.1 * atmos[5] * atmos[5])
    temp_diff = 3.0 * (atmos[2] - ocean[2])
    humid_diff = 0.002 * (atmos[3] - ocean[3])
    height = 10.0 * jnp.exp(0.3 * atmos[4])
    log_moment = jnp.log(height * 10000.0) - 0.5 * ocean[4]
    log_heat = jnp.log(height * 10000.0) - 0.5 * ocean[5]
    root_moment = KAPPA / log_moment
    root_heat = KAPPA / log_heat
    for sweep in range(ITERS):
        friction = root_moment * wind_speed
        buoyancy = root_heat * (temp_diff / 290.0 + 0.61 * humid_diff)
        stability = jnp.clip(KAPPA * GRAVITY * height * buoyancy / (friction * friction), -10.0, 3.0)
        unstable = jnp.sqrt(jnp.sqrt(1.0 - 16.0 * jnp.minimum(stability, 0.0)))
        psi_moment = jnp.where(stability > 0.0, -5.0 * stability, 2.0 * jnp.log((1.0 + unstable) / 2.0) + jnp.log((1.0 + unstable * unstable) / 2.0) - 2.0 * jnp.arctan(unstable) + jnp.pi / 2.0)
        psi_heat = jnp.where(stability > 0.0, -5.0 * stability, 2.0 * jnp.log((1.0 + unstable * unstable) / 2.0))
        root_moment = 0.5 * root_moment + 0.5 * KAPPA / (log_moment - psi_moment)
        root_heat = 0.5 * root_heat + 0.5 * KAPPA / (log_heat - psi_heat)
    drag = FLUX_SCALE * root_moment * root_moment * wind_speed
    transfer = FLUX_SCALE * root_moment * root_heat * wind_speed
    leading = jnp.stack([drag * shear_x, drag * shear_y, transfer * temp_diff, 500.0 * transfer * humid_diff])
    tracer = transfer[None, :] * (atmos[6:] - ocean[6:])
    return jnp.concatenate([leading, tracer], axis=0)

def locate(refs, send_list, owner, blocks_dev):
    slot = refs // 128
    lane = refs % 128
    neighbor = slot // CAP
    within = slot % CAP
    offset_x = neighbor // 3 - 1
    offset_y = neighbor % 3 - 1
    source = (owner // N_GY - offset_x) % N_GX * N_GY + (owner % N_GY - offset_y) % N_GY
    block = send_list[source, neighbor, within]
    return (source * blocks_dev * 128 + block * 128 + lane).astype(jnp.int32)

def reference(atmosphere_surface_fields, ocean_surface_fields, atm_area, ocn_area, send_atm, send_ocn, atm_ref, ocn_ref, cell_area, cell_mask, cell_count):
    owners = jnp.arange(OWNERS).astype(jnp.int32)
    local_index = jnp.arange(XC_DEV).astype(jnp.int32)

    def visit(carry, item):
        atm_sum, ocn_sum = carry
        owner, atm_refs, ocn_refs, areas, masks, live_count = item
        atm_cols = locate(atm_refs, send_atm, owner, A_BLK_DEV)
        ocn_cols = locate(ocn_refs, send_ocn, owner, O_BLK_DEV)
        fluxes = surface_flux(atmosphere_surface_fields[:, atm_cols], ocean_surface_fields[:, ocn_cols])
        weight = jnp.where((local_index < live_count) & (masks == 1), areas, 0.0 * areas)
        area_weighted_flux = fluxes * weight[None, :]
        return ((atm_sum.at[:, atm_cols].add(area_weighted_flux), ocn_sum.at[:, ocn_cols].add(area_weighted_flux)), None)
    start = (jnp.zeros((FR, NA), jnp.float32), jnp.zeros((FR, NO), jnp.float32))
    items = (owners, atm_ref.reshape(OWNERS, XC_DEV), ocn_ref.reshape(OWNERS, XC_DEV), cell_area.reshape(OWNERS, XC_DEV), cell_mask.reshape(OWNERS, XC_DEV), cell_count)
    (atm_sum, ocn_sum), unused = lax.scan(visit, start, items)
    return (atm_sum / atm_area[None, :], ocn_sum / ocn_area[None, :])
```

```python
import functools

import jax
import jax.numpy as jnp
import numpy as np
from jax import lax
from jax.experimental import pallas as pl
from jax.experimental.pallas import tpu as pltpu
from jax.sharding import PartitionSpec as P

ITERS = 6
GRP = 32
LANES = 128
CAP = 24
SLOTS = 9 * CAP
FIELDS = (6, 7, 7)
SUMS = (4, 7, 7)

VMEM = pl.BlockSpec(memory_space=pltpu.VMEM)
SMEM = pl.BlockSpec(memory_space=pltpu.SMEM)
F32 = jnp.float32
BF16 = jnp.bfloat16


def call(body, name, out_shape, in_specs, scratch=(), us=10):
    return pl.pallas_call(
        body,
        name=name,
        out_shape=out_shape,
        in_specs=in_specs,
        out_specs=jax.tree.map(lambda _: VMEM, out_shape),
        scratch_shapes=list(scratch),
        compiler_params=pltpu.CompilerParams(vmem_limit_bytes=40 * 1024 * 1024),
        cost_estimate=pl.CostEstimate(flops=0, bytes_accessed=int(us * 3.3e6), transcendentals=0),
    )


def shape(*dims):
    return jax.ShapeDtypeStruct(dims, F32)


def pack_body(ids_a, ids_o, fields_a, fields_o, *outs):
    for n in range(9):
        p, q = n // 3, n % 3

        def step(c, _):
            for comp, (ids, fields) in enumerate(((ids_a, fields_a), (ids_o, fields_o))):
                col = pl.ds(pl.multiple_of(jnp.maximum(ids[n * CAP + c], 0) * LANES, LANES), LANES)
                top, mid, low = fields[0:8, col], fields[8:16, col], fields[16:20, col]
                block = (p * 2 + comp) * CAP + c
                outs[q][pl.ds(block * 6, 6), :] = top[:6]
                outs[3 + q][pl.ds(block * 7, 2), :] = top[6:]
                outs[3 + q][pl.ds(block * 7 + 2, 5), :] = mid[:5]
                outs[6 + q][pl.ds(block * 7, 3), :] = mid[5:]
                outs[6 + q][pl.ds(block * 7 + 3, 4), :] = low
            return 0

        lax.fori_loop(0, CAP, step, 0, unroll=8)


def pack(ids_a, ids_o, fields_a, fields_o):
    outs = tuple(shape(3 * 2 * CAP * f, LANES) for f in FIELDS for _ in range(3))
    return call(pack_body, "pack", outs, [SMEM, SMEM, VMEM, VMEM], us=4)(ids_a, ids_o, fields_a, fields_o)


def hop(value, axis, steps):
    count = lax.axis_size(axis)
    return lax.ppermute(value, axis, [(s, (s + steps) % count) for s in range(count)])


def third(value, k):
    size = value.shape[0] // 3
    return value[k * size : (k + 1) * size]


def to_owners(parts):
    came = [hop(parts[0], "gy", -1), parts[1], hop(parts[2], "gy", 1)]
    ahead = hop(jnp.concatenate([third(v, 2) for v in came]), "gx", 1)
    behind = hop(jnp.concatenate([third(v, 0) for v in came]), "gx", -1)
    return behind, ahead, came


def to_sources(parts):
    came = [hop(parts[0], "gx", 1), parts[1], hop(parts[2], "gx", -1)]
    up = hop(jnp.concatenate([third(v, 2) for v in came]), "gy", -1)
    down = hop(jnp.concatenate([third(v, 0) for v in came]), "gy", 1)
    return down, up, came


def join_slabs(pieces, slabs, rows):
    behind, ahead, *came = pieces
    for p in range(3):
        for q in range(3):
            for comp in range(2):
                if p == 1:
                    source, at = came[q], (2 + comp) * rows
                else:
                    source, at = (behind, None, ahead)[p], (q * 2 + comp) * rows
                slabs[comp][pl.ds((p * 3 + q) * rows, rows), :] = source[pl.ds(at, rows), :]


def take_lanes(v, index):
    dims = lax.GatherDimensionNumbers(
        offset_dims=(),
        collapsed_slice_dims=(1,),
        start_index_map=(1,),
        operand_batching_dims=(0,),
        start_indices_batching_dims=(0,),
    )
    return lax.gather(v, index[..., None], dims, (1, 1), mode=lax.GatherScatterMode.PROMISE_IN_BOUNDS)


def gather_row(slab, slots, r, stride, lanes, quarter):
    out = None
    index = jnp.broadcast_to(lanes, (8, LANES))
    for j in range(4):
        v = take_lanes(slab[pl.ds(slots[4 * r + j] * stride, 8), :], index)
        out = v if out is None else jnp.where(quarter >= j, v, out)
    return out


def odd_arctan_coefficients():
    z_top = 0.325
    nodes = (np.cos((np.arange(400) + 0.5) * np.pi / 400) + 1) / 2 * z_top
    t = np.sqrt(nodes)
    fit = np.polynomial.chebyshev.Chebyshev.fit(nodes, np.arctan(t) / t, 7, domain=[0, z_top])
    return [float(c) for c in fit.convert(kind=np.polynomial.Polynomial).coef]


ARCTAN = odd_arctan_coefficients()


def small_arctan(t):
    z = t * t
    total = jnp.full_like(t, ARCTAN[-1])
    for c in ARCTAN[-2::-1]:
        total = total * z + c
    return t * total


def bulk(a, o):
    shear_x = 6.0 * a[0] - 0.3 * o[0]
    shear_y = 6.0 * a[1] - 0.3 * o[1]
    speed2 = shear_x * shear_x + shear_y * shear_y + 0.25 + 0.1 * a[5] * a[5]
    speed = jnp.sqrt(speed2)
    dtemp = 3.0 * (a[2] - o[2])
    dhum = 0.002 * (a[3] - o[3])
    height = 10.0 * jnp.exp(0.3 * a[4])
    log_height = jnp.log(height * 10000.0)
    log_m = log_height - 0.5 * o[4]
    log_h = log_height - 0.5 * o[5]
    rm = 0.4 / log_m
    rh = 0.4 / log_h
    base = (0.4 * 9.8) * height * (dtemp / 290.0 + 0.61 * dhum) / speed2
    for _ in range(ITERS):
        zeta = jnp.clip(base * rh / (rm * rm), -10.0, 3.0)
        u2 = jnp.sqrt(1.0 - 16.0 * jnp.minimum(zeta, 0.0))
        u = jnp.sqrt(u2)
        one_u = 1.0 + u
        one_u2 = 1.0 + u2
        stable = -5.0 * zeta
        psi_m = jnp.where(
            zeta > 0.0,
            stable,
            jnp.log(one_u * one_u * one_u2 * 0.125) - 2.0 * small_arctan((u - 1.0) / one_u),
        )
        psi_h = jnp.where(zeta > 0.0, stable, 2.0 * jnp.log(one_u2 * 0.5))
        rm = 0.5 * rm + 0.2 / (log_m - psi_m)
        rh = 0.5 * rh + 0.2 / (log_h - psi_h)
    drag = 25.0 * rm * rm * speed
    transfer = 25.0 * rm * rh * speed
    return (drag * shear_x, drag * shear_y, transfer * dtemp, 500.0 * transfer * dhum), transfer


def onehots(lanes_a, lanes_o, column):
    one, zero = jnp.ones((), BF16), jnp.zeros((), BF16)
    a = jnp.where(column == lanes_a.astype(BF16), one, zero)
    o = jnp.where(column == lanes_o.astype(BF16), one, zero)
    return jnp.concatenate([a, o], axis=0)


def two_pieces(v):
    high = v.astype(BF16).astype(F32)
    return high, v - high


def scatter_row(v, lanes_a, lanes_o, column, quarter):
    parts = [jnp.where(quarter == j, x, 0.0) for j in range(4) for x in two_pieces(v)]
    left = jnp.concatenate(parts, axis=0).astype(BF16)
    right = onehots(lanes_a, lanes_o, column)
    sums = lax.dot_general(left, right, (((1,), (1,)), ((), ())), preferred_element_type=F32)
    return [sums[16 * j : 16 * j + 8] + sums[16 * j + 8 : 16 * j + 16] for j in range(4)]


def add_groups(sums, slots_a, slots_o, r, acc_a, acc_o):
    for j in range(4):
        at_a = pl.ds(pl.multiple_of(slots_a[4 * r + j] * 8, 8), 8)
        at_o = pl.ds(pl.multiple_of(slots_o[4 * r + j] * 8, 8), 8)
        acc_a[at_a, :] += sums[j][:, :LANES]
        acc_o[at_o, :] += sums[j][:, LANES:]


def split_sums(accs, outs, rows):
    for p in range(3):
        for q in range(3):

            def step(c, _):
                for comp in range(2):
                    at = pl.multiple_of(((p * 3 + q) * CAP + c) * 8, 8)
                    outs[p][pl.ds(((q * 2 + comp) * CAP + c) * rows, rows), :] = accs[comp][pl.ds(at, 8), :][:rows]
                return 0

            lax.fori_loop(0, CAP, step, 0, unroll=8)


def iota_quarter():
    return lax.broadcasted_iota(jnp.int32, (8, LANES), 1) // GRP


def iota_column():
    return lax.broadcasted_iota(jnp.int32, (LANES, LANES), 0).astype(BF16)


def first_body(nrows, count, slots_a, slots_o, ref_a, ref_o, area, mask, *rest):
    pieces, (weight, lead, slab_a, slab_o, cells_a, cells_o) = rest[:5], rest[5:]
    join_slabs(pieces, (slab_a, slab_o), CAP * 6)
    quarter = iota_quarter()

    def gather(r, _):
        for ref, slab, slots, cells in ((ref_a, slab_a, slots_a, cells_a), (ref_o, slab_o, slots_o, cells_o)):
            lanes = ref[pl.ds(r, 1), :] & (LANES - 1)
            cells[pl.ds(r, 8, stride=nrows), :] = gather_row(slab, slots, r, 6, lanes, quarter)
        return 0

    lax.fori_loop(0, nrows, gather, 0, unroll=32)
    live = count[0]
    depth = 64

    def iterate(i, _):
        row = pl.multiple_of(i * depth, depth)
        a = [cells_a[pl.ds(pl.multiple_of(f * nrows + row, depth), depth), :] for f in range(6)]
        o = [cells_o[pl.ds(pl.multiple_of(f * nrows + row, depth), depth), :] for f in range(6)]
        here = pl.ds(row, depth)
        place = (row + lax.broadcasted_iota(jnp.int32, (depth, LANES), 0)) * LANES
        place = place + lax.broadcasted_iota(jnp.int32, (depth, LANES), 1)
        w = jnp.where((place < live) & (mask[here, :] == 1), area[here, :], 0.0)
        fluxes, transfer = bulk(a, o)
        weight[here, :] = transfer * w
        for k, flux in enumerate(fluxes):
            lead[pl.ds(row * 4 + k, depth, stride=4), :] = flux * w
        return 0

    lax.fori_loop(0, nrows // depth, iterate, 0)


def first(count, slots, refs, area, mask, pieces):
    nrows = area.shape[0]
    return call(
        functools.partial(first_body, nrows),
        "bulk",
        (shape(nrows, LANES), shape(nrows * 4 + 8, LANES)),
        [SMEM] * 3 + [VMEM] * 9,
        [pltpu.VMEM((SLOTS * 6 + 8, LANES), F32)] * 2 + [pltpu.VMEM((8 * nrows, LANES), F32)] * 2,
        us=20,
    )(count, *slots, *refs, area, mask, *pieces)


def lead_body(nrows, slots_a, slots_o, ref_a, ref_o, lead, *rest):
    outs, accs = rest[:3], rest[3:]
    for acc in accs:
        acc[...] = jnp.zeros_like(acc)
    quarter, column = iota_quarter(), iota_column()

    def step(r, _):
        lanes_a, lanes_o = ref_a[pl.ds(r, 1), :] & (LANES - 1), ref_o[pl.ds(r, 1), :] & (LANES - 1)
        v = lead[pl.ds(r * 4, 8), :]
        add_groups(scatter_row(v, lanes_a, lanes_o, column, quarter), slots_a, slots_o, r, *accs)
        return 0

    lax.fori_loop(0, nrows, step, 0, unroll=32)
    split_sums(accs, outs, 4)


def lead_sums(slots, refs, lead):
    nrows = refs[0].shape[0]
    return call(
        functools.partial(lead_body, nrows),
        "lead",
        tuple(shape(3 * 2 * CAP * 4, LANES) for _ in range(3)),
        [SMEM] * 2 + [VMEM] * 3,
        [pltpu.VMEM((SLOTS * 8, LANES), F32)] * 2,
        us=12,
    )(*slots, *refs, lead)


def tracer_body(nrows, slots_a, slots_o, ref_a, ref_o, weight, *rest):
    pieces, outs, slabs, accs = rest[:5], rest[5:8], rest[8:10], rest[10:]
    join_slabs(pieces, slabs, CAP * 7)
    for acc in accs:
        acc[...] = jnp.zeros_like(acc)
    quarter, column = iota_quarter(), iota_column()

    def step(r, _):
        lanes_a, lanes_o = ref_a[pl.ds(r, 1), :] & (LANES - 1), ref_o[pl.ds(r, 1), :] & (LANES - 1)
        a = gather_row(slabs[0], slots_a, r, 7, lanes_a, quarter)
        o = gather_row(slabs[1], slots_o, r, 7, lanes_o, quarter)
        v = (a - o) * jnp.broadcast_to(weight[pl.ds(r, 1), :], (8, LANES))
        add_groups(scatter_row(v, lanes_a, lanes_o, column, quarter), slots_a, slots_o, r, *accs)
        return 0

    lax.fori_loop(0, nrows, step, 0, unroll=32)
    split_sums(accs, outs, 7)


def tracers(slots, refs, weight, pieces):
    nrows = weight.shape[0]
    return call(
        functools.partial(tracer_body, nrows),
        "tracers",
        tuple(shape(3 * 2 * CAP * 7, LANES) for _ in range(3)),
        [SMEM] * 2 + [VMEM] * 8,
        [pltpu.VMEM((SLOTS * 7 + 8, LANES), F32)] * 2 + [pltpu.VMEM((SLOTS * 8, LANES), F32)] * 2,
        us=18,
    )(*slots, *refs, weight, *pieces)


def unpack_body(nblocks, ids_a, ids_o, area_a, area_o, *rest):
    parts = [rest[5 * k : 5 * k + 5] for k in range(3)]
    outs, accs = rest[15:17], rest[17:]
    for acc in accs:
        acc[...] = jnp.zeros_like(acc)
    for n in range(9):
        p, q = n // 3, n % 3

        def step(c, _):
            for comp, ids in enumerate((ids_a, ids_o)):
                at = pl.ds(pl.multiple_of(jnp.maximum(ids[n * CAP + c], 0) * 8, 8), 8)
                for k, rows in enumerate(SUMS):
                    down, up, *came = parts[k]
                    if q == 1:
                        source, base = came[p], (2 + comp) * CAP
                    else:
                        source, base = (down, None, up)[q], (p * 2 + comp) * CAP
                    acc = accs[comp * 3 + k]
                    acc[pl.ds(at.start, rows), :] += source[pl.ds((base + c) * rows, rows), :]
            return 0

        lax.fori_loop(0, CAP, step, 0, unroll=8)

    def finish(b, _):
        col = pl.ds(pl.multiple_of(b * LANES, LANES), LANES)
        for comp, area in enumerate((area_a, area_o)):
            row = 0
            for k, rows in enumerate(SUMS):
                v = accs[comp * 3 + k][pl.ds(pl.multiple_of(b * 8, 8), 8), :] / area[pl.ds(b, 1), :]
                outs[comp][row : row + rows, col] = v[:rows]
                row += rows
        return 0

    lax.fori_loop(0, nblocks, finish, 0, unroll=8)


def unpack(ids_a, ids_o, area_a, area_o, parts):
    nblocks = area_a.shape[0]
    flat = [x for part in parts for x in part]
    return call(
        functools.partial(unpack_body, nblocks),
        "unpack",
        (shape(sum(SUMS), nblocks * LANES),) * 2,
        [SMEM] * 2 + [VMEM] * 17,
        [pltpu.VMEM((nblocks * 8, LANES), F32)] * 6,
        us=6,
    )(ids_a, ids_o, area_a, area_o, *flat)


def shards(fields_a, fields_o, area_a, area_o, send_a, send_o, atm_ref, ocn_ref, cell_area, cell_mask, cell_count):
    ids_a, ids_o = send_a.reshape(-1), send_o.reshape(-1)
    packed = pack(ids_a, ids_o, fields_a, fields_o)
    refs = (atm_ref.reshape(-1, LANES), ocn_ref.reshape(-1, LANES))
    slots = tuple(ref[:, ::GRP].reshape(-1) // LANES for ref in refs)
    came = []
    for k in range(3):
        behind, ahead, rest = to_owners(packed[3 * k : 3 * k + 3])
        came.append((behind, ahead, *rest))
    weight, lead = first(
        cell_count, slots, refs, cell_area.reshape(-1, LANES), cell_mask.reshape(-1, LANES), came[0]
    )
    sums = [lead_sums(slots, refs, lead)] + [tracers(slots, refs, weight, came[k]) for k in (1, 2)]
    back = []
    for part in sums:
        down, up, rest = to_sources(part)
        back.append((down, up, *rest))
    return unpack(ids_a, ids_o, area_a.reshape(-1, LANES), area_o.reshape(-1, LANES), back)


def solution(mesh):
    both = ("gx", "gy")
    in_specs = (P(None, both), P(None, both), P(both), P(both), P(both, None, None), P(both, None, None)) + (P(both),) * 5
    return jax.shard_map(shards, mesh=mesh, in_specs=in_specs, out_specs=(P(None, both),) * 2, check_vma=False)
```

```python
import functools

import jax
import jax.numpy as jnp
import numpy as np
from jax import lax
from jax.experimental import pallas as pl
from jax.experimental.pallas import tpu as pltpu
from jax.sharding import PartitionSpec as P

ITERS = 6
GRP = 32
LANES = 128
CAP = 24
SLOTS = 9 * CAP
LEAD = 6
TRACERS = 14
FLUXES = 18
NEIGHBOURS = ((0, 1), (0, -1), (1, 1), (-1, -1), (-1, 1), (1, -1), (1, 0), (-1, 0))

VMEM = pl.BlockSpec(memory_space=pltpu.VMEM)
SMEM = pl.BlockSpec(memory_space=pltpu.SMEM)
F32 = jnp.float32
BF16 = jnp.bfloat16


def cost(us):
    return pl.CostEstimate(flops=0, bytes_accessed=int(us * 3.3e6), transcendentals=0)


def call(body, name, out_shape, in_specs, scratch=(), us=10):
    return pl.pallas_call(
        body,
        name=name,
        out_shape=out_shape,
        in_specs=in_specs,
        out_specs=jax.tree.map(lambda _: VMEM, out_shape),
        scratch_shapes=list(scratch),
        compiler_params=pltpu.CompilerParams(vmem_limit_bytes=40 * 1024 * 1024),
        cost_estimate=cost(us),
    )


def shape(*dims):
    return jax.ShapeDtypeStruct(dims, F32)


def block_column(ids, n, c):
    return pl.ds(pl.multiple_of(jnp.maximum(ids[n, 0, c], 0) * LANES, LANES), LANES)


def pack_lead_body(ids_a, ids_o, fields_a, fields_o, *rest):
    outs, tops, sems = rest[:3], rest[3:5], rest[5]
    copies = [
        pltpu.make_async_copy(fields.at[pl.ds(0, 8), :], top, sems.at[k])
        for k, (fields, top) in enumerate(zip((fields_a, fields_o), tops))
    ]
    for copy in copies:
        copy.start()
    for copy in copies:
        copy.wait()
    for n in range(9):
        p, q = n // 3, n % 3

        def step(c, _):
            for comp, (ids, top) in enumerate(zip((ids_a, ids_o), tops)):
                v = top[:, block_column(ids, n, c)]
                outs[q][pl.ds(((p * 2 + comp) * CAP + c) * LEAD, LEAD), :] = v[:LEAD]
            return 0

        lax.fori_loop(0, CAP, step, 0, unroll=CAP)


def pack_lead(ids_a, ids_o, fields_a, fields_o):
    hbm = pl.BlockSpec(memory_space=pltpu.HBM)
    return call(
        pack_lead_body,
        "pack_lead",
        (shape(3 * 2 * CAP * LEAD, LANES),) * 3,
        [SMEM, SMEM, hbm, hbm],
        [pltpu.VMEM((8, fields_a.shape[1]), F32)] * 2 + [pltpu.SemaphoreType.DMA((2,))],
        us=2,
    )(ids_a, ids_o, fields_a, fields_o)


def pack_tracers_body(ids_a, ids_o, fields_a, fields_o, *outs):
    for n in range(9):
        p, q = n // 3, n % 3

        def step(c, _):
            for comp, (ids, fields) in enumerate(((ids_a, fields_a), (ids_o, fields_o))):
                col = block_column(ids, n, c)
                row = ((q * 2 + comp) * CAP + c) * TRACERS
                outs[p][pl.ds(row, 2), :] = fields[0:8, col][6:]
                outs[p][pl.ds(row + 2, 8), :] = fields[8:16, col]
                outs[p][pl.ds(row + 10, 4), :] = fields[16:20, col]
            return 0

        lax.fori_loop(0, CAP, step, 0, unroll=8)


def pack_tracers(ids_a, ids_o, fields_a, fields_o):
    outs = (shape(3 * 2 * CAP * TRACERS, LANES),) * 3
    return call(pack_tracers_body, "pack_tracers", outs, [SMEM, SMEM, VMEM, VMEM], us=4)(ids_a, ids_o, fields_a, fields_o)


def hop(value, axis, steps):
    count = lax.axis_size(axis)
    return lax.ppermute(value, axis, [(s, (s + steps) % count) for s in range(count)])


def send(value, p, q):
    nx, ny = lax.axis_size("gx"), lax.axis_size("gy")
    pairs = [(x * ny + y, (x + p) % nx * ny + (y + q) % ny) for x in range(nx) for y in range(ny)]
    return lax.ppermute(value, ("gx", "gy"), pairs)


def exchange(values, sign):
    out = list(values)
    for p, q in NEIGHBOURS:
        n = (p + 1) * 3 + q + 1
        out[n] = send(values[n], sign * p, sign * q)
    return out


def third(value, k):
    size = value.shape[0] // 3
    return value[k * size : (k + 1) * size]


def to_owners(lead, tracers):
    lead = [hop(lead[0], "gy", -1), lead[1], hop(lead[2], "gy", 1)]
    tracers_x = [hop(tracers[0], "gx", -1), tracers[1], hop(tracers[2], "gx", 1)]
    lead[0], lead[2], _ = lax.optimization_barrier((lead[0], lead[2], tracers[1]))
    ahead = hop(jnp.concatenate([third(v, 2) for v in lead]), "gx", 1)
    behind = hop(jnp.concatenate([third(v, 0) for v in lead]), "gx", -1)
    up = hop(jnp.concatenate([third(v, 2) for v in tracers_x]), "gy", 1)
    down = hop(jnp.concatenate([third(v, 0) for v in tracers_x]), "gy", -1)
    return (behind, ahead, *lead), (down, up, *tracers_x)


def join_slabs(pieces, slabs, rows):
    behind, ahead, *came = pieces
    for p in range(3):
        for q in range(3):
            for comp in range(2):
                if p == 1:
                    source, at = came[q], (2 + comp) * rows
                else:
                    source, at = (behind, None, ahead)[p], (q * 2 + comp) * rows
                slabs[comp][pl.ds((p * 3 + q) * rows, rows), :] = source[pl.ds(at, rows), :]


def take_lanes(v, index):
    dims = lax.GatherDimensionNumbers(
        offset_dims=(),
        collapsed_slice_dims=(1,),
        start_index_map=(1,),
        operand_batching_dims=(0,),
        start_indices_batching_dims=(0,),
    )
    return lax.gather(v, index[..., None], dims, (1, 1), mode=lax.GatherScatterMode.PROMISE_IN_BOUNDS)


def gather_row(slab, slots, r, stride, first, lanes, quarter):
    out = None
    index = jnp.broadcast_to(lanes, (8, LANES))
    for j in range(4):
        v = take_lanes(slab[pl.ds(slots[j, r] * stride + first, 8), :], index)
        out = v if out is None else jnp.where(quarter >= j, v, out)
    return out


def odd_arctan_coefficients():
    z_top = 0.325
    nodes = (np.cos((np.arange(400) + 0.5) * np.pi / 400) + 1) / 2 * z_top
    t = np.sqrt(nodes)
    fit = np.polynomial.chebyshev.Chebyshev.fit(nodes, np.arctan(t) / t, 7, domain=[0, z_top])
    return [float(c) for c in fit.convert(kind=np.polynomial.Polynomial).coef]


ARCTAN = odd_arctan_coefficients()


def small_arctan(t):
    z = t * t
    total = jnp.full_like(t, ARCTAN[-1])
    for c in ARCTAN[-2::-1]:
        total = total * z + c
    return t * total


def bulk(a, o):
    shear_x = 6.0 * a[0] - 0.3 * o[0]
    shear_y = 6.0 * a[1] - 0.3 * o[1]
    speed2 = shear_x * shear_x + shear_y * shear_y + 0.25 + 0.1 * a[5] * a[5]
    speed = jnp.sqrt(speed2)
    dtemp = 3.0 * (a[2] - o[2])
    dhum = 0.002 * (a[3] - o[3])
    height = 10.0 * jnp.exp(0.3 * a[4])
    log_height = jnp.log(height * 10000.0)
    log_m = log_height - 0.5 * o[4]
    log_h = log_height - 0.5 * o[5]
    rm = 0.4 / log_m
    rh = 0.4 / log_h
    base = (0.4 * 9.8) * height * (dtemp / 290.0 + 0.61 * dhum) / speed2
    for _ in range(ITERS):
        zeta = jnp.clip(base * rh / (rm * rm), -10.0, 3.0)
        u2 = jnp.sqrt(1.0 - 16.0 * jnp.minimum(zeta, 0.0))
        u = jnp.sqrt(u2)
        one_u = 1.0 + u
        one_u2 = 1.0 + u2
        stable = -5.0 * zeta
        psi_m = jnp.where(
            zeta > 0.0,
            stable,
            jnp.log(one_u * one_u * one_u2 * 0.125) - 2.0 * small_arctan((u - 1.0) / one_u),
        )
        psi_h = jnp.where(zeta > 0.0, stable, 2.0 * jnp.log(one_u2 * 0.5))
        rm = 0.5 * rm + 0.2 / (log_m - psi_m)
        rh = 0.5 * rh + 0.2 / (log_h - psi_h)
    drag = 25.0 * rm * rm * speed
    transfer = 25.0 * rm * rh * speed
    return (drag * shear_x, drag * shear_y, transfer * dtemp, 500.0 * transfer * dhum), transfer


def onehots(lanes_a, lanes_o, column):
    one, zero = jnp.ones((), BF16), jnp.zeros((), BF16)
    a = jnp.where(column == lanes_a.astype(BF16), one, zero)
    o = jnp.where(column == lanes_o.astype(BF16), one, zero)
    return jnp.concatenate([a, o], axis=0)


def two_pieces(v):
    high = v.astype(BF16).astype(F32)
    return high, v - high


def scatter_row(values, lanes_a, lanes_o, column, quarter):
    pieces = [x for v in values for x in two_pieces(v)]
    left = jnp.concatenate([jnp.where(quarter == j, x, 0.0) for j in range(4) for x in pieces], axis=0).astype(BF16)
    right = onehots(lanes_a, lanes_o, column)
    sums = lax.dot_general(left, right, (((1,), (1,)), ((), ())), preferred_element_type=F32)
    rows = 16 * len(values)
    return [
        [sums[rows * j + 16 * k : rows * j + 16 * k + 8] + sums[rows * j + 16 * k + 8 : rows * j + 16 * k + 16] for k in range(len(values))]
        for j in range(4)
    ]


def add_groups(sums, slots_a, slots_o, r, acc_a, acc_o):
    for j in range(4):
        base_a, base_o = slots_a[j, r] * 24, slots_o[j, r] * 24
        for k, x in enumerate(sums[j]):
            acc_a[pl.ds(pl.multiple_of(base_a + 8 * k, 8), 8), :] += x[:, :LANES]
            acc_o[pl.ds(pl.multiple_of(base_o + 8 * k, 8), 8), :] += x[:, LANES:]


def slots_body(ref_a, ref_o, out_a, out_o):
    pick = jnp.where(
        lax.broadcasted_iota(jnp.int32, (8, LANES), 1) == GRP * lax.broadcasted_iota(jnp.int32, (8, LANES), 0), 1.0, 0.0
    ).astype(BF16)
    for ref, out in ((ref_a, out_a), (ref_o, out_o)):
        slot = (ref[...] >> 7).astype(F32).astype(BF16)
        picked = lax.dot_general(pick, slot, (((1,), (1,)), ((), ())), preferred_element_type=F32)
        out[...] = picked.astype(jnp.int32)


def group_slots(refs):
    out = (jax.ShapeDtypeStruct((8, refs[0].shape[0]), jnp.int32),) * 2
    return call(slots_body, "slots", out, [VMEM, VMEM], us=1)(*refs)


def iota_quarter():
    return lax.broadcasted_iota(jnp.int32, (8, LANES), 1) // GRP


def iota_column():
    return lax.broadcasted_iota(jnp.int32, (LANES, LANES), 0).astype(BF16)


def first_body(nrows, count, slots_a, slots_o, ref_a, ref_o, area, mask, *rest):
    pieces, (weight, lead, slab_a, slab_o, cells_a, cells_o) = rest[:5], rest[5:]
    join_slabs(pieces, (slab_a, slab_o), CAP * LEAD)
    quarter = iota_quarter()

    def gather(r, _):
        for ref, slab, slots, cells in ((ref_a, slab_a, slots_a, cells_a), (ref_o, slab_o, slots_o, cells_o)):
            lanes = ref[pl.ds(r, 1), :] & (LANES - 1)
            cells[pl.ds(r, 8, stride=nrows), :] = gather_row(slab, slots, r, LEAD, 0, lanes, quarter)
        return 0

    lax.fori_loop(0, nrows, gather, 0, unroll=32)
    live = count[0]
    depth = 64

    def iterate(i, _):
        row = pl.multiple_of(i * depth, depth)
        a = [cells_a[pl.ds(pl.multiple_of(f * nrows + row, depth), depth), :] for f in range(6)]
        o = [cells_o[pl.ds(pl.multiple_of(f * nrows + row, depth), depth), :] for f in range(6)]
        here = pl.ds(row, depth)
        place = (row + lax.broadcasted_iota(jnp.int32, (depth, LANES), 0)) * LANES
        place = place + lax.broadcasted_iota(jnp.int32, (depth, LANES), 1)
        w = jnp.where((place < live) & (mask[here, :] == 1), area[here, :], 0.0)
        fluxes, transfer = bulk(a, o)
        weight[here, :] = transfer * w
        for k, flux in enumerate(fluxes):
            lead[pl.ds(row * 4 + k, depth, stride=4), :] = flux * w
        return 0

    lax.fori_loop(0, nrows // depth, iterate, 0)


def first(count, slots, refs, area, mask, pieces):
    nrows = area.shape[0]
    return call(
        functools.partial(first_body, nrows),
        "bulk",
        (shape(nrows, LANES), shape(nrows * 4 + 8, LANES)),
        [SMEM] * 3 + [VMEM] * 9,
        [pltpu.VMEM((SLOTS * LEAD + 8, LANES), F32)] * 2 + [pltpu.VMEM((8 * nrows, LANES), F32)] * 2,
        us=20,
    )(count, *slots, *refs, area, mask, *pieces)


def scatter_body(nrows, slots_a, slots_o, ref_a, ref_o, weight, lead, *rest):
    (down, up, *came), outs, slabs, accs = rest[:5], rest[5:14], rest[14:16], rest[16:]
    size = CAP * TRACERS
    for n in range(9):
        p, q = n // 3, n % 3
        for comp in range(2):
            source, at = (came[p], 2 + comp) if q == 1 else ((down, None, up)[q], p * 2 + comp)
            slabs[comp][pl.ds(n * size, size), :] = source[pl.ds(at * size, size), :]
    for acc in accs:
        acc[...] = jnp.zeros_like(acc)
    quarter, column = iota_quarter(), iota_column()

    def step(r, _):
        lanes_a, lanes_o = ref_a[pl.ds(r, 1), :] & (LANES - 1), ref_o[pl.ds(r, 1), :] & (LANES - 1)
        w = jnp.broadcast_to(weight[pl.ds(r, 1), :], (8, LANES))
        values = [lead[pl.ds(r * 4, 8), :]]
        for at in (0, 8):
            a = gather_row(slabs[0], slots_a, r, TRACERS, at, lanes_a, quarter)
            o = gather_row(slabs[1], slots_o, r, TRACERS, at, lanes_o, quarter)
            values.append((a - o) * w)
        add_groups(scatter_row(values, lanes_a, lanes_o, column, quarter), slots_a, slots_o, r, *accs)
        return 0

    lax.fori_loop(0, nrows, step, 0, unroll=32)
    for n in range(9):

        def split(c, _):
            for comp in range(2):
                at = pl.multiple_of((n * CAP + c) * 24, 8)
                to = (comp * CAP + c) * FLUXES
                outs[n][pl.ds(to, 4), :] = accs[comp][pl.ds(at, 8), :][:4]
                outs[n][pl.ds(to + 4, 8), :] = accs[comp][pl.ds(at + 8, 8), :]
                outs[n][pl.ds(to + 12, 6), :] = accs[comp][pl.ds(at + 16, 8), :][:6]
            return 0

        lax.fori_loop(0, CAP, split, 0, unroll=8)


def scatter(slots, refs, weight, lead, pieces):
    nrows = weight.shape[0]
    return call(
        functools.partial(scatter_body, nrows),
        "scatter",
        (shape(2 * CAP * FLUXES, LANES),) * 9,
        [SMEM] * 2 + [VMEM] * 9,
        [pltpu.VMEM((SLOTS * TRACERS + 8, LANES), F32)] * 2 + [pltpu.VMEM((SLOTS * 24, LANES), F32)] * 2,
        us=22,
    )(*slots, *refs, weight, lead, *pieces)


def unpack_body(nblocks, ids_a, ids_o, area_a, area_o, *rest):
    parts, outs, accs = rest[:9], rest[9:11], rest[11:]
    for acc in accs:
        acc[...] = jnp.zeros_like(acc)
    for n in range(9):

        def step(c, _):
            for comp, ids in enumerate((ids_a, ids_o)):
                at = pl.multiple_of(jnp.maximum(ids[n, 0, c], 0) * 24, 8)
                base = (comp * CAP + c) * FLUXES
                for first, rows in ((0, 8), (8, 8), (16, 2)):
                    accs[comp][pl.ds(at + first, rows), :] += parts[n][pl.ds(base + first, rows), :]
            return 0

        lax.fori_loop(0, CAP, step, 0, unroll=8)

    def finish(b, _):
        col = pl.ds(pl.multiple_of(b * LANES, LANES), LANES)
        at = pl.multiple_of(b * 24, 8)
        for comp, area in enumerate((area_a, area_o)):
            for first, rows in ((0, 8), (8, 8), (16, 2)):
                outs[comp][first : first + rows, col] = accs[comp][pl.ds(at + first, rows), :] / area[pl.ds(b, 1), :]
        return 0

    lax.fori_loop(0, nblocks, finish, 0, unroll=8)


def unpack(ids_a, ids_o, area_a, area_o, parts):
    nblocks = area_a.shape[0]
    return call(
        functools.partial(unpack_body, nblocks),
        "unpack",
        (shape(FLUXES, nblocks * LANES),) * 2,
        [SMEM] * 2 + [VMEM] * 11,
        [pltpu.VMEM((nblocks * 24, LANES), F32)] * 2,
        us=5,
    )(ids_a, ids_o, area_a, area_o, *parts)


def shards(fields_a, fields_o, area_a, area_o, send_a, send_o, atm_ref, ocn_ref, cell_area, cell_mask, cell_count):
    refs = (atm_ref.reshape(-1, LANES), ocn_ref.reshape(-1, LANES))
    send_a, send_o = send_a.transpose(1, 0, 2), send_o.transpose(1, 0, 2)
    lead = list(pack_lead(send_a, send_o, fields_a, fields_o))
    lead[1], ids_a, ids_o = lax.optimization_barrier((lead[1], send_a, send_o))
    lead_came, came = to_owners(lead, pack_tracers(ids_a, ids_o, fields_a, fields_o))
    slots = group_slots(refs)
    weight, led = first(cell_count, slots, refs, cell_area.reshape(-1, LANES), cell_mask.reshape(-1, LANES), lead_came)
    back = exchange(scatter(slots, refs, weight, led, came), -1)
    return unpack(send_a, send_o, area_a.reshape(-1, LANES), area_o.reshape(-1, LANES), back)


def solution(mesh):
    both = ("gx", "gy")
    in_specs = (P(None, both), P(None, both), P(both), P(both), P(both, None, None), P(both, None, None)) + (P(both),) * 5
    return jax.shard_map(shards, mesh=mesh, in_specs=in_specs, out_specs=(P(None, both),) * 2, check_vma=False)
```

```python
import functools

import jax
import jax.numpy as jnp
import numpy as np
from jax import lax
from jax.experimental import pallas as pl
from jax.experimental.pallas import tpu as pltpu
from jax.sharding import PartitionSpec as P

ITERS = 6
GRP = 32
LANES = 128
CAP = 24
SLOTS = 9 * CAP
LEAD = 6
TRACERS = 14
FLUXES = 18
MIDDLE = 8
OUTER = 10

HBM = pl.BlockSpec(memory_space=pltpu.HBM)
VMEM = pl.BlockSpec(memory_space=pltpu.VMEM)
SMEM = pl.BlockSpec(memory_space=pltpu.SMEM)
F32 = jnp.float32
BF16 = jnp.bfloat16


def cost(us):
    return pl.CostEstimate(flops=0, bytes_accessed=int(us * 3.3e6), transcendentals=0)


def call(body, name, out_shape, in_specs, scratch=(), us=10, limit=40, out_space=VMEM):
    return pl.pallas_call(
        body,
        name=name,
        out_shape=out_shape,
        in_specs=in_specs,
        out_specs=jax.tree.map(lambda _: out_space, out_shape),
        scratch_shapes=list(scratch),
        compiler_params=pltpu.CompilerParams(vmem_limit_bytes=limit * 1024 * 1024),
        cost_estimate=cost(us),
    )


def shape(*dims):
    return jax.ShapeDtypeStruct(dims, F32)


def block_column(ids, n, c):
    return pl.ds(pl.multiple_of(jnp.maximum(ids[n, 0, c], 0) * LANES, LANES), LANES)


def pack_body(send_a, send_o, fields_a, fields_o, *rest):
    outs, (ids_a, ids_o, top_a, top_o, low_a, low_o), held, in_sems, out_sems = (
        rest[:6],
        rest[6:12],
        rest[12:18],
        rest[18],
        rest[19],
    )
    lead, tracers = held[:3], held[3:]
    count = fields_a.shape[0]
    moves = [(send_a, ids_a), (send_o, ids_o)]
    moves += [(f.at[pl.ds(0, 8), :], to) for f, to in ((fields_a, top_a), (fields_o, top_o))]
    moves += [(f.at[pl.ds(8, count - 8), :], to) for f, to in ((fields_a, low_a), (fields_o, low_o))]
    copies = [pltpu.make_async_copy(source, to, in_sems.at[k]) for k, (source, to) in enumerate(moves)]
    leave = [pltpu.make_async_copy(source, to, out_sems.at[k]) for k, (source, to) in enumerate(zip(held, outs))]
    for copy in copies:
        copy.start()
    for copy in copies[:4]:
        copy.wait()
    sides = ((ids_a, top_a, low_a), (ids_o, top_o, low_o))
    for n in range(9):
        p, q = n // 3, n % 3

        def lead_step(c, _):
            for comp, (ids, top, _) in enumerate(sides):
                v = top[:, block_column(ids, n, c)]
                lead[q][pl.ds(((p * 2 + comp) * CAP + c) * LEAD, LEAD), :] = v[:LEAD]
                tracers[p][pl.ds(((q * 2 + comp) * CAP + c) * TRACERS, 2), :] = v[LEAD:]
            return 0

        lax.fori_loop(0, CAP, lead_step, 0, unroll=CAP)
    for copy in leave[:3]:
        copy.start()
    for copy in copies[4:]:
        copy.wait()
    for n in range(9):
        p, q = n // 3, n % 3

        def step(c, _):
            for comp, (ids, _, low) in enumerate(sides):
                col = block_column(ids, n, c)
                row = ((q * 2 + comp) * CAP + c) * TRACERS + 2
                tracers[p][pl.ds(row, 8), :] = low[0:8, col]
                tracers[p][pl.ds(row + 8, 4), :] = low[8:12, col]
            return 0

        lax.fori_loop(0, CAP, step, 0, unroll=CAP)
        if q == 2:
            leave[3 + p].start()
    for copy in leave:
        copy.wait()


def pack(send_a, send_o, fields_a, fields_o):
    count, columns = fields_a.shape
    outs = (shape(3 * 2 * CAP * LEAD, LANES),) * 3 + (shape(3 * 2 * CAP * TRACERS, LANES),) * 3
    outs = call(
        pack_body,
        "pack",
        outs,
        [HBM] * 4,
        [pltpu.SMEM(send_a.shape, jnp.int32)] * 2
        + [pltpu.VMEM((8, columns), F32)] * 2
        + [pltpu.VMEM((count - 8, columns), F32)] * 2
        + [pltpu.VMEM(o.shape, F32) for o in outs]
        + [pltpu.SemaphoreType.DMA((6,))] * 2,
        us=4,
        limit=63,
        out_space=HBM,
    )(send_a, send_o, fields_a, fields_o)
    return outs[:3], outs[3:]


def hop(value, axis, steps):
    count = lax.axis_size(axis)
    return lax.ppermute(value, axis, [(s, (s + steps) % count) for s in range(count)])


def third(value, k):
    size = value.shape[0] // 3
    return value[k * size : (k + 1) * size]


def two_ways(y_first, x_first, sign):
    y = [hop(y_first[0], "gy", -sign), y_first[1], hop(y_first[2], "gy", sign)]
    x = [hop(x_first[0], "gx", -sign), x_first[1], hop(x_first[2], "gx", sign)]
    sides = [jnp.concatenate([third(v, k) for v in x]) for k in (0, 2)]
    *_, y[0], y[2] = lax.optimization_barrier((*sides, y[0], y[2]))
    ends = [jnp.concatenate([third(v, k) for v in y]) for k in (0, 2)]
    behind, ahead = hop(ends[0], "gx", -sign), hop(ends[1], "gx", sign)
    down, up = hop(sides[0], "gy", -sign), hop(sides[1], "gy", sign)
    return (behind, ahead, *y), (down, up, *x)


def y_first_rows(pieces, p, q, comp, size):
    behind, ahead, *came = pieces
    if p == 1:
        return came[q], (2 + comp) * size
    return (behind, None, ahead)[p], (q * 2 + comp) * size


def x_first_rows(pieces, p, q, comp, size):
    down, up, *came = pieces
    if q == 1:
        return came[p], (2 + comp) * size
    return (down, None, up)[q], (p * 2 + comp) * size


def join_slabs(find, pieces, slabs, rows):
    for n in range(9):
        for comp in range(2):
            source, at = find(pieces, n // 3, n % 3, comp, rows)
            slabs[comp][pl.ds(n * rows, rows), :] = source[pl.ds(at, rows), :]


def take_lanes(v, index):
    dims = lax.GatherDimensionNumbers(
        offset_dims=(),
        collapsed_slice_dims=(1,),
        start_index_map=(1,),
        operand_batching_dims=(0,),
        start_indices_batching_dims=(0,),
    )
    return lax.gather(v, index[..., None], dims, (1, 1), mode=lax.GatherScatterMode.PROMISE_IN_BOUNDS)


def gather_row(slab, slots, r, stride, first, lanes, quarter):
    out = None
    index = jnp.broadcast_to(lanes, (8, LANES))
    for j in range(4):
        v = take_lanes(slab[pl.ds(slots[j, r] * stride + first, 8), :], index)
        out = v if out is None else jnp.where(quarter >= j, v, out)
    return out


def odd_arctan_coefficients():
    z_top = 0.325
    nodes = (np.cos((np.arange(400) + 0.5) * np.pi / 400) + 1) / 2 * z_top
    t = np.sqrt(nodes)
    fit = np.polynomial.chebyshev.Chebyshev.fit(nodes, np.arctan(t) / t, 7, domain=[0, z_top])
    return [float(c) for c in fit.convert(kind=np.polynomial.Polynomial).coef]


ARCTAN = odd_arctan_coefficients()


def small_arctan(t):
    z = t * t
    total = jnp.full_like(t, ARCTAN[-1])
    for c in ARCTAN[-2::-1]:
        total = total * z + c
    return t * total


def bulk(a, o):
    shear_x = 6.0 * a[0] - 0.3 * o[0]
    shear_y = 6.0 * a[1] - 0.3 * o[1]
    speed2 = shear_x * shear_x + shear_y * shear_y + 0.25 + 0.1 * a[5] * a[5]
    speed = jnp.sqrt(speed2)
    dtemp = 3.0 * (a[2] - o[2])
    dhum = 0.002 * (a[3] - o[3])
    height = 10.0 * jnp.exp(0.3 * a[4])
    log_height = jnp.log(height * 10000.0)
    log_m = log_height - 0.5 * o[4]
    log_h = log_height - 0.5 * o[5]
    rm = 0.4 / log_m
    rh = 0.4 / log_h
    base = (0.4 * 9.8) * height * (dtemp / 290.0 + 0.61 * dhum) / speed2
    for _ in range(ITERS):
        zeta = jnp.clip(base * rh / (rm * rm), -10.0, 3.0)
        u2 = jnp.sqrt(1.0 - 16.0 * jnp.minimum(zeta, 0.0))
        u = jnp.sqrt(u2)
        one_u = 1.0 + u
        one_u2 = 1.0 + u2
        stable = -5.0 * zeta
        psi_m = jnp.where(
            zeta > 0.0,
            stable,
            jnp.log(one_u * one_u * one_u2 * 0.125) - 2.0 * small_arctan((u - 1.0) / one_u),
        )
        psi_h = jnp.where(zeta > 0.0, stable, 2.0 * jnp.log(one_u2 * 0.5))
        rm = 0.5 * rm + 0.2 / (log_m - psi_m)
        rh = 0.5 * rh + 0.2 / (log_h - psi_h)
    drag = 25.0 * rm * rm * speed
    transfer = 25.0 * rm * rh * speed
    return (drag * shear_x, drag * shear_y, transfer * dtemp, 500.0 * transfer * dhum), transfer


def onehots(lanes_a, lanes_o, column):
    one, zero = jnp.ones((), BF16), jnp.zeros((), BF16)
    a = jnp.where(column == lanes_a.astype(BF16), one, zero)
    o = jnp.where(column == lanes_o.astype(BF16), one, zero)
    return jnp.concatenate([a, o], axis=0)


def two_pieces(v):
    high = v.astype(BF16).astype(F32)
    return high, v - high


def scatter_row(values, lanes_a, lanes_o, column, quarter):
    def masked(v):
        return [jnp.where(quarter == j, v, 0.0) for j in range(4)]

    halves = []
    for pieces in zip(*(two_pieces(v) for v in values)):
        lead, one, two = map(masked, pieces)
        halves.append(jnp.concatenate([x for pair in zip(one, two) for x in pair] + lead, axis=0).astype(BF16))
    left = jnp.concatenate(halves, axis=1)
    right = onehots(lanes_a, lanes_o, column)
    right = jnp.concatenate([right, right], axis=1)
    sums = lax.dot_general(left, right, (((1,), (1,)), ((), ())), preferred_element_type=F32)
    return [[sums[at : at + 8] for at in (64 + 8 * j, 16 * j, 16 * j + 8)] for j in range(4)]


def add_groups(sums, slots_a, slots_o, r, acc_a, acc_o):
    for j in range(4):
        base_a, base_o = slots_a[j, r] * 24, slots_o[j, r] * 24
        for k, x in enumerate(sums[j]):
            acc_a[pl.ds(pl.multiple_of(base_a + 8 * k, 8), 8), :] += x[:, :LANES]
            acc_o[pl.ds(pl.multiple_of(base_o + 8 * k, 8), 8), :] += x[:, LANES:]


def slots_body(ref_a, ref_o, out_a, out_o):
    pick = jnp.where(
        lax.broadcasted_iota(jnp.int32, (8, LANES), 1) == GRP * lax.broadcasted_iota(jnp.int32, (8, LANES), 0), 1.0, 0.0
    ).astype(BF16)
    for ref, out in ((ref_a, out_a), (ref_o, out_o)):
        slot = (ref[...] >> 7).astype(F32).astype(BF16)
        picked = lax.dot_general(pick, slot, (((1,), (1,)), ((), ())), preferred_element_type=F32)
        out[...] = picked.astype(jnp.int32)


def group_slots(refs):
    out = (jax.ShapeDtypeStruct((8, refs[0].shape[0]), jnp.int32),) * 2
    return call(slots_body, "slots", out, [VMEM, VMEM], us=1)(*refs)


def iota_quarter():
    return lax.broadcasted_iota(jnp.int32, (8, LANES), 1) // GRP


def iota_column():
    return lax.broadcasted_iota(jnp.int32, (LANES, LANES), 0).astype(BF16)


def first_body(nrows, count, slots_a, slots_o, ref_a, ref_o, area, mask, *rest):
    pieces, (weight, lead, slab_a, slab_o, cells_a, cells_o) = rest[:5], rest[5:]
    join_slabs(y_first_rows, pieces, (slab_a, slab_o), CAP * LEAD)
    quarter = iota_quarter()

    def gather(r, _):
        for ref, slab, slots, cells in ((ref_a, slab_a, slots_a, cells_a), (ref_o, slab_o, slots_o, cells_o)):
            lanes = ref[pl.ds(r, 1), :] & (LANES - 1)
            cells[pl.ds(r, 8, stride=nrows), :] = gather_row(slab, slots, r, LEAD, 0, lanes, quarter)
        return 0

    lax.fori_loop(0, nrows, gather, 0, unroll=64)
    live = count[0]
    depth = 64

    def iterate(i, _):
        row = pl.multiple_of(i * depth, depth)
        a = [cells_a[pl.ds(pl.multiple_of(f * nrows + row, depth), depth), :] for f in range(6)]
        o = [cells_o[pl.ds(pl.multiple_of(f * nrows + row, depth), depth), :] for f in range(6)]
        here = pl.ds(row, depth)
        place = (row + lax.broadcasted_iota(jnp.int32, (depth, LANES), 0)) * LANES
        place = place + lax.broadcasted_iota(jnp.int32, (depth, LANES), 1)
        w = jnp.where((place < live) & (mask[here, :] == 1), area[here, :], 0.0)
        fluxes, transfer = bulk(a, o)
        weight[here, :] = transfer * w
        for k, flux in enumerate(fluxes):
            lead[pl.ds(row * 4 + k, depth, stride=4), :] = flux * w
        return 0

    lax.fori_loop(0, nrows // depth, iterate, 0)


def first(count, slots, refs, area, mask, pieces):
    nrows = area.shape[0]
    return call(
        functools.partial(first_body, nrows),
        "bulk",
        (shape(nrows, LANES), shape(nrows * 4 + 8, LANES)),
        [SMEM] * 3 + [VMEM] * 9,
        [pltpu.VMEM((SLOTS * LEAD + 8, LANES), F32)] * 2 + [pltpu.VMEM((8 * nrows, LANES), F32)] * 2,
        us=20,
    )(count, *slots, *refs, area, mask, *pieces)


def scatter_body(nrows, slots_a, slots_o, ref_a, ref_o, weight, lead, *rest):
    pieces, middle, outer, slabs, accs = rest[:5], rest[5:8], rest[8:11], rest[11:13], rest[13:]
    join_slabs(x_first_rows, pieces, slabs, CAP * TRACERS)
    for acc in accs:
        acc[...] = jnp.zeros_like(acc)
    quarter, column = iota_quarter(), iota_column()

    def step(r, _):
        lanes_a, lanes_o = ref_a[pl.ds(r, 1), :] & (LANES - 1), ref_o[pl.ds(r, 1), :] & (LANES - 1)
        w = jnp.broadcast_to(weight[pl.ds(r, 1), :], (8, LANES))
        values = [lead[pl.ds(r * 4, 8), :]]
        for at in (0, 8):
            a = gather_row(slabs[0], slots_a, r, TRACERS, at, lanes_a, quarter)
            o = gather_row(slabs[1], slots_o, r, TRACERS, at, lanes_o, quarter)
            values.append((a - o) * w)
        add_groups(scatter_row(values, lanes_a, lanes_o, column, quarter), slots_a, slots_o, r, *accs)
        return 0

    lax.fori_loop(0, nrows, step, 0, unroll=64)
    for n in range(9):
        p, q = n // 3, n % 3

        def split(c, _):
            for comp in range(2):
                at = pl.multiple_of((n * CAP + c) * 24, 8)
                to = pl.multiple_of(((p * 2 + comp) * CAP + c) * MIDDLE, 8)
                middle[q][pl.ds(to, MIDDLE), :] = accs[comp][pl.ds(at + 8, 8), :]
                to = ((q * 2 + comp) * CAP + c) * OUTER
                outer[p][pl.ds(to, 4), :] = accs[comp][pl.ds(at, 8), :][:4]
                outer[p][pl.ds(to + 4, 6), :] = accs[comp][pl.ds(at + 16, 8), :][:6]
            return 0

        lax.fori_loop(0, CAP, split, 0, unroll=8)


def scatter(slots, refs, weight, lead, pieces):
    nrows = weight.shape[0]
    return call(
        functools.partial(scatter_body, nrows),
        "scatter",
        (shape(3 * 2 * CAP * MIDDLE, LANES),) * 3 + (shape(3 * 2 * CAP * OUTER, LANES),) * 3,
        [SMEM] * 2 + [VMEM] * 9,
        [pltpu.VMEM((SLOTS * TRACERS + 8, LANES), F32)] * 2 + [pltpu.VMEM((SLOTS * 24, LANES), F32)] * 2,
        us=22,
    )(*slots, *refs, weight, lead, *pieces)


def add_middle_body(send_a, send_o, *rest):
    pieces, accs, (ids_a, ids_o, sems) = rest[:5], rest[5:7], rest[7:]
    copies = [pltpu.make_async_copy(s, to, sems.at[k]) for k, (s, to) in enumerate(((send_a, ids_a), (send_o, ids_o)))]
    for copy in copies:
        copy.start()
    for acc in accs:
        acc[...] = jnp.zeros_like(acc)
    for copy in copies:
        copy.wait()
    for n in range(9):

        def step(c, _):
            for comp, ids in enumerate((ids_a, ids_o)):
                at = pl.multiple_of(jnp.maximum(ids[n, 0, c], 0) * MIDDLE, 8)
                source, first = y_first_rows(pieces, n // 3, n % 3, comp, CAP)
                accs[comp][pl.ds(at, 8), :] += source[pl.ds(pl.multiple_of((first + c) * MIDDLE, 8), 8), :]
            return 0

        lax.fori_loop(0, CAP, step, 0, unroll=CAP)


def add_middle(send_a, send_o, nblocks, pieces):
    return call(
        add_middle_body,
        "add_middle",
        (shape(nblocks * MIDDLE, LANES),) * 2,
        [HBM] * 2 + [VMEM] * 5,
        [pltpu.SMEM(send_a.shape, jnp.int32)] * 2 + [pltpu.SemaphoreType.DMA((2,))],
        us=2,
    )(send_a, send_o, *pieces)


def unpack_body(nblocks, send_a, send_o, area_a, area_o, middle_a, middle_o, *rest):
    pieces, outs, accs, held, (ids_a, ids_o, sems, out_sems) = rest[:5], rest[5:7], rest[7:9], rest[9:11], rest[11:]
    copies = [pltpu.make_async_copy(s, to, sems.at[k]) for k, (s, to) in enumerate(((send_a, ids_a), (send_o, ids_o)))]
    for copy in copies:
        copy.start()
    for acc in accs:
        acc[...] = jnp.zeros_like(acc)
    for copy in copies:
        copy.wait()
    for n in range(9):

        def step(c, _):
            for comp, ids in enumerate((ids_a, ids_o)):
                at = pl.multiple_of(jnp.maximum(ids[n, 0, c], 0) * 16, 8)
                source, first = x_first_rows(pieces, n // 3, n % 3, comp, CAP)
                accs[comp][pl.ds(at, 8), :] += source[pl.ds((first + c) * OUTER, 8), :]
                accs[comp][pl.ds(at + 8, 2), :] += source[pl.ds((first + c) * OUTER + 8, 2), :]
            return 0

        lax.fori_loop(0, CAP, step, 0, unroll=CAP)
    quarters = 4
    size = nblocks // quarters
    leave = []
    for k in range(quarters):

        def finish(b, _):
            col = pl.ds(pl.multiple_of(b * LANES, LANES), LANES)
            for comp, (area, middle) in enumerate(((area_a, middle_a), (area_o, middle_o))):
                scale = 1.0 / area[pl.ds(b, 1), :]
                held[comp][0:4, col] = accs[comp][pl.ds(b * 16, 4), :] * scale
                held[comp][4:8, col] = middle[pl.ds(b * MIDDLE, 4), :] * scale
                held[comp][8:12, col] = middle[pl.ds(b * MIDDLE + 4, 4), :] * scale
                held[comp][12:16, col] = accs[comp][pl.ds(b * 16 + 4, 4), :] * scale
                held[comp][16:18, col] = accs[comp][pl.ds(b * 16 + 8, 2), :] * scale
            return 0

        lax.fori_loop(k * size, (k + 1) * size, finish, 0, unroll=8)
        here = pl.ds(k * size * LANES, size * LANES)
        for comp in range(2):
            copy = pltpu.make_async_copy(held[comp].at[:, here], outs[comp].at[:, here], out_sems.at[2 * k + comp])
            copy.start()
            leave.append(copy)
    for copy in leave:
        copy.wait()


def unpack(send_a, send_o, area_a, area_o, middle, outer):
    nblocks = area_a.shape[0]
    columns = nblocks * LANES
    return call(
        functools.partial(unpack_body, nblocks),
        "unpack",
        (shape(FLUXES, columns),) * 2,
        [HBM] * 2 + [VMEM] * 9,
        [pltpu.VMEM((nblocks * 16, LANES), F32)] * 2
        + [pltpu.VMEM((FLUXES, columns), F32)] * 2
        + [pltpu.SMEM(send_a.shape, jnp.int32)] * 2
        + [pltpu.SemaphoreType.DMA((2,)), pltpu.SemaphoreType.DMA((8,))],
        us=4,
        out_space=HBM,
    )(send_a, send_o, area_a, area_o, *add_middle(send_a, send_o, nblocks, middle), *outer)


def shards(fields_a, fields_o, area_a, area_o, send_a, send_o, atm_ref, ocn_ref, cell_area, cell_mask, cell_count):
    refs = (atm_ref.reshape(-1, LANES), ocn_ref.reshape(-1, LANES))
    send_a, send_o = send_a.transpose(1, 0, 2), send_o.transpose(1, 0, 2)
    lead_came, came = two_ways(*pack(send_a, send_o, fields_a, fields_o), 1)
    slots = group_slots(refs)
    weight, led = first(cell_count, slots, refs, cell_area.reshape(-1, LANES), cell_mask.reshape(-1, LANES), lead_came)
    sums = scatter(slots, refs, weight, led, came)
    middle, outer = two_ways(sums[:3], sums[3:], -1)
    return unpack(send_a, send_o, area_a.reshape(-1, LANES), area_o.reshape(-1, LANES), middle, outer)


def solution(mesh):
    both = ("gx", "gy")
    in_specs = (P(None, both), P(None, both), P(both), P(both), P(both, None, None), P(both, None, None)) + (P(both),) * 5
    return jax.shard_map(shards, mesh=mesh, in_specs=in_specs, out_specs=(P(None, both),) * 2, check_vma=False)
```

```python
import functools

import jax
import jax.numpy as jnp
import numpy as np
from jax import lax
from jax.experimental import pallas as pl
from jax.experimental.pallas import tpu as pltpu
from jax.sharding import PartitionSpec as P

ITERS = 6
GRP = 32
LANES = 128
CAP = 24
SLOTS = 9 * CAP
LEAD = 6
TRACERS = 14
FLUXES = 18
MIDDLE = 8
OUTER = 10

HBM = pl.BlockSpec(memory_space=pltpu.HBM)
VMEM = pl.BlockSpec(memory_space=pltpu.VMEM)
SMEM = pl.BlockSpec(memory_space=pltpu.SMEM)
F32 = jnp.float32
BF16 = jnp.bfloat16


def cost(us):
    return pl.CostEstimate(flops=0, bytes_accessed=int(us * 3.3e6), transcendentals=0)


def call(body, name, out_shape, in_specs, scratch=(), us=10, limit=40, out_space=VMEM):
    return pl.pallas_call(
        body,
        name=name,
        out_shape=out_shape,
        in_specs=in_specs,
        out_specs=jax.tree.map(lambda _: out_space, out_shape),
        scratch_shapes=list(scratch),
        compiler_params=pltpu.CompilerParams(vmem_limit_bytes=limit * 1024 * 1024),
        cost_estimate=cost(us),
    )


def shape(*dims):
    return jax.ShapeDtypeStruct(dims, F32)


def block_column(ids, n, c):
    return pl.ds(pl.multiple_of(jnp.maximum(ids[n, 0, c], 0) * LANES, LANES), LANES)


def pack_body(send_a, send_o, fields_a, fields_o, *rest):
    outs, (ids_a, ids_o, top_a, top_o, low_a, low_o), held, in_sems, out_sems = (
        rest[:6],
        rest[6:12],
        rest[12:18],
        rest[18],
        rest[19],
    )
    lead, tracers = held[:3], held[3:]
    count = fields_a.shape[0]
    moves = [(send_a, ids_a), (send_o, ids_o)]
    moves += [(f.at[pl.ds(0, 8), :], to) for f, to in ((fields_a, top_a), (fields_o, top_o))]
    moves += [(f.at[pl.ds(8, count - 8), :], to) for f, to in ((fields_a, low_a), (fields_o, low_o))]
    copies = [pltpu.make_async_copy(source, to, in_sems.at[k]) for k, (source, to) in enumerate(moves)]
    leave = [pltpu.make_async_copy(source, to, out_sems.at[k]) for k, (source, to) in enumerate(zip(held, outs))]
    for copy in copies:
        copy.start()
    for copy in copies[:4]:
        copy.wait()
    sides = ((ids_a, top_a, low_a), (ids_o, top_o, low_o))
    for n in range(9):
        p, q = n // 3, n % 3

        def lead_step(c, _):
            for comp, (ids, top, _) in enumerate(sides):
                v = top[:, block_column(ids, n, c)]
                lead[q][pl.ds(((p * 2 + comp) * CAP + c) * LEAD, LEAD), :] = v[:LEAD]
                tracers[p][pl.ds(((q * 2 + comp) * CAP + c) * TRACERS, 2), :] = v[LEAD:]
            return 0

        lax.fori_loop(0, CAP, lead_step, 0, unroll=CAP)
    for copy in leave[:3]:
        copy.start()
    for copy in copies[4:]:
        copy.wait()
    for n in range(9):
        p, q = n // 3, n % 3

        def step(c, _):
            for comp, (ids, _, low) in enumerate(sides):
                col = block_column(ids, n, c)
                row = ((q * 2 + comp) * CAP + c) * TRACERS + 2
                tracers[p][pl.ds(row, 8), :] = low[0:8, col]
                tracers[p][pl.ds(row + 8, 4), :] = low[8:12, col]
            return 0

        lax.fori_loop(0, CAP, step, 0, unroll=CAP)
        if q == 2:
            leave[3 + p].start()
    for copy in leave:
        copy.wait()


def pack(send_a, send_o, fields_a, fields_o):
    count, columns = fields_a.shape
    outs = (shape(3 * 2 * CAP * LEAD, LANES),) * 3 + (shape(3 * 2 * CAP * TRACERS, LANES),) * 3
    outs = call(
        pack_body,
        "pack",
        outs,
        [HBM] * 4,
        [pltpu.SMEM(send_a.shape, jnp.int32)] * 2
        + [pltpu.VMEM((8, columns), F32)] * 2
        + [pltpu.VMEM((count - 8, columns), F32)] * 2
        + [pltpu.VMEM(o.shape, F32) for o in outs]
        + [pltpu.SemaphoreType.DMA((6,))] * 2,
        us=4,
        limit=63,
        out_space=HBM,
    )(send_a, send_o, fields_a, fields_o)
    return outs[:3], outs[3:]


def hop(value, axis, steps):
    count = lax.axis_size(axis)
    return lax.ppermute(value, axis, [(s, (s + steps) % count) for s in range(count)])


def third(value, k):
    size = value.shape[0] // 3
    return value[k * size : (k + 1) * size]


def two_ways(y_first, x_first, sign):
    y = [hop(y_first[0], "gy", -sign), y_first[1], hop(y_first[2], "gy", sign)]
    x = [hop(x_first[0], "gx", -sign), x_first[1], hop(x_first[2], "gx", sign)]
    sides = [jnp.concatenate([third(v, k) for v in x]) for k in (0, 2)]
    *_, y[0], y[2] = lax.optimization_barrier((*sides, y[0], y[2]))
    ends = [jnp.concatenate([third(v, k) for v in y]) for k in (0, 2)]
    behind, ahead = hop(ends[0], "gx", -sign), hop(ends[1], "gx", sign)
    down, up = hop(sides[0], "gy", -sign), hop(sides[1], "gy", sign)
    return (behind, ahead, *y), (down, up, *x)


def y_first_rows(pieces, p, q, comp, size):
    behind, ahead, *came = pieces
    if p == 1:
        return came[q], (2 + comp) * size
    return (behind, None, ahead)[p], (q * 2 + comp) * size


def x_first_rows(pieces, p, q, comp, size):
    down, up, *came = pieces
    if q == 1:
        return came[p], (2 + comp) * size
    return (down, None, up)[q], (p * 2 + comp) * size


def join_slabs(find, pieces, slabs, rows):
    for n in range(9):
        for comp in range(2):
            source, at = find(pieces, n // 3, n % 3, comp, rows)
            slabs[comp][pl.ds(n * rows, rows), :] = source[pl.ds(at, rows), :]


def take_lanes(v, index):
    dims = lax.GatherDimensionNumbers(
        offset_dims=(),
        collapsed_slice_dims=(1,),
        start_index_map=(1,),
        operand_batching_dims=(0,),
        start_indices_batching_dims=(0,),
    )
    return lax.gather(v, index[..., None], dims, (1, 1), mode=lax.GatherScatterMode.PROMISE_IN_BOUNDS)


def gather_row(slab, slots, r, stride, first, lanes, quarter):
    out = None
    index = jnp.broadcast_to(lanes, (8, LANES))
    for j in range(4):
        v = take_lanes(slab[pl.ds(slots[j, r] * stride + first, 8), :], index)
        out = v if out is None else jnp.where(quarter >= j, v, out)
    return out


def odd_arctan_coefficients():
    z_top = 0.325
    nodes = (np.cos((np.arange(400) + 0.5) * np.pi / 400) + 1) / 2 * z_top
    t = np.sqrt(nodes)
    fit = np.polynomial.chebyshev.Chebyshev.fit(nodes, np.arctan(t) / t, 7, domain=[0, z_top])
    return [float(c) for c in fit.convert(kind=np.polynomial.Polynomial).coef]


ARCTAN = odd_arctan_coefficients()


def small_arctan(t):
    z = t * t
    total = jnp.full_like(t, ARCTAN[-1])
    for c in ARCTAN[-2::-1]:
        total = total * z + c
    return t * total


def bulk(a, o):
    shear_x = 6.0 * a[0] - 0.3 * o[0]
    shear_y = 6.0 * a[1] - 0.3 * o[1]
    speed2 = shear_x * shear_x + shear_y * shear_y + 0.25 + 0.1 * a[5] * a[5]
    speed = jnp.sqrt(speed2)
    dtemp = 3.0 * (a[2] - o[2])
    dhum = 0.002 * (a[3] - o[3])
    height = 10.0 * jnp.exp(0.3 * a[4])
    log_height = jnp.log(height * 10000.0)
    log_m = log_height - 0.5 * o[4]
    log_h = log_height - 0.5 * o[5]
    rm = 0.4 / log_m
    rh = 0.4 / log_h
    base = (0.4 * 9.8) * height * (dtemp / 290.0 + 0.61 * dhum) / speed2
    for _ in range(ITERS):
        zeta = jnp.clip(base * rh / (rm * rm), -10.0, 3.0)
        u2 = jnp.sqrt(1.0 - 16.0 * jnp.minimum(zeta, 0.0))
        u = jnp.sqrt(u2)
        one_u = 1.0 + u
        one_u2 = 1.0 + u2
        stable = -5.0 * zeta
        psi_m = jnp.where(
            zeta > 0.0,
            stable,
            jnp.log(one_u * one_u * one_u2 * 0.125) - 2.0 * small_arctan((u - 1.0) / one_u),
        )
        psi_h = jnp.where(zeta > 0.0, stable, 2.0 * jnp.log(one_u2 * 0.5))
        rm = 0.5 * rm + 0.2 / (log_m - psi_m)
        rh = 0.5 * rh + 0.2 / (log_h - psi_h)
    drag = 25.0 * rm * rm * speed
    transfer = 25.0 * rm * rh * speed
    return (drag * shear_x, drag * shear_y, transfer * dtemp, 500.0 * transfer * dhum), transfer


def onehots(lanes_a, lanes_o, column):
    one, zero = jnp.ones((), BF16), jnp.zeros((), BF16)
    a = jnp.where(column == lanes_a.astype(BF16), one, zero)
    o = jnp.where(column == lanes_o.astype(BF16), one, zero)
    return jnp.concatenate([a, o], axis=0)


def two_pieces(v):
    high = v.astype(BF16).astype(F32)
    return high, v - high


def scatter_row(values, lanes_a, lanes_o, column, quarter):
    def masked(v):
        return [jnp.where(quarter == j, v, 0.0) for j in range(4)]

    halves = []
    for pieces in zip(*(two_pieces(v) for v in values)):
        lead, one, two = map(masked, pieces)
        halves.append(jnp.concatenate([x for pair in zip(one, two) for x in pair] + lead, axis=0).astype(BF16))
    left = jnp.concatenate(halves, axis=1)
    right = onehots(lanes_a, lanes_o, column)
    right = jnp.concatenate([right, right], axis=1)
    sums = lax.dot_general(left, right, (((1,), (1,)), ((), ())), preferred_element_type=F32)
    return [[sums[at : at + 8] for at in (64 + 8 * j, 16 * j, 16 * j + 8)] for j in range(4)]


def add_groups(sums, slots_a, slots_o, r, acc_a, acc_o):
    for j in range(4):
        base_a, base_o = slots_a[j, r] * 24, slots_o[j, r] * 24
        for k, x in enumerate(sums[j]):
            acc_a[pl.ds(pl.multiple_of(base_a + 8 * k, 8), 8), :] += x[:, :LANES]
            acc_o[pl.ds(pl.multiple_of(base_o + 8 * k, 8), 8), :] += x[:, LANES:]


def slots_body(ref_a, ref_o, out_a, out_o):
    pick = jnp.where(
        lax.broadcasted_iota(jnp.int32, (8, LANES), 1) == GRP * lax.broadcasted_iota(jnp.int32, (8, LANES), 0), 1.0, 0.0
    ).astype(BF16)
    for ref, out in ((ref_a, out_a), (ref_o, out_o)):
        slot = (ref[...] >> 7).astype(F32).astype(BF16)
        picked = lax.dot_general(pick, slot, (((1,), (1,)), ((), ())), preferred_element_type=F32)
        out[...] = picked.astype(jnp.int32)


def group_slots(refs):
    out = (jax.ShapeDtypeStruct((8, refs[0].shape[0]), jnp.int32),) * 2
    return call(slots_body, "slots", out, [VMEM, VMEM], us=1)(*refs)


def iota_quarter():
    return lax.broadcasted_iota(jnp.int32, (8, LANES), 1) // GRP


def iota_column():
    return lax.broadcasted_iota(jnp.int32, (LANES, LANES), 0).astype(BF16)


def first_body(nrows, count, slots_a, slots_o, ref_a, ref_o, area, mask, *rest):
    pieces, (weight, lead, slab_a, slab_o, cells_a, cells_o) = rest[:5], rest[5:]
    join_slabs(y_first_rows, pieces, (slab_a, slab_o), CAP * LEAD)
    quarter = iota_quarter()

    def gather(r, _):
        for ref, slab, slots, cells in ((ref_a, slab_a, slots_a, cells_a), (ref_o, slab_o, slots_o, cells_o)):
            lanes = ref[pl.ds(r, 1), :] & (LANES - 1)
            cells[pl.ds(r, 8, stride=nrows), :] = gather_row(slab, slots, r, LEAD, 0, lanes, quarter)
        return 0

    lax.fori_loop(0, nrows, gather, 0, unroll=128)
    live = count[0]
    depth = 64

    def iterate(i, _):
        row = pl.multiple_of(i * depth, depth)
        a = [cells_a[pl.ds(pl.multiple_of(f * nrows + row, depth), depth), :] for f in range(6)]
        o = [cells_o[pl.ds(pl.multiple_of(f * nrows + row, depth), depth), :] for f in range(6)]
        here = pl.ds(row, depth)
        place = (row + lax.broadcasted_iota(jnp.int32, (depth, LANES), 0)) * LANES
        place = place + lax.broadcasted_iota(jnp.int32, (depth, LANES), 1)
        w = jnp.where((place < live) & (mask[here, :] == 1), area[here, :], 0.0)
        fluxes, transfer = bulk(a, o)
        weight[here, :] = transfer * w
        for k, flux in enumerate(fluxes):
            lead[pl.ds(row * 4 + k, depth, stride=4), :] = flux * w
        return 0

    lax.fori_loop(0, nrows // depth, iterate, 0)


def first(count, slots, refs, area, mask, pieces):
    nrows = area.shape[0]
    return call(
        functools.partial(first_body, nrows),
        "bulk",
        (shape(nrows, LANES), shape(nrows * 4 + 8, LANES)),
        [SMEM] * 3 + [VMEM] * 9,
        [pltpu.VMEM((SLOTS * LEAD + 8, LANES), F32)] * 2 + [pltpu.VMEM((8 * nrows, LANES), F32)] * 2,
        us=20,
    )(count, *slots, *refs, area, mask, *pieces)


def scatter_body(nrows, slots_a, slots_o, ref_a, ref_o, weight, lead, *rest):
    pieces, middle, outer, slabs, accs = rest[:5], rest[5:8], rest[8:11], rest[11:13], rest[13:]
    join_slabs(x_first_rows, pieces, slabs, CAP * TRACERS)
    for acc in accs:
        acc[...] = jnp.zeros_like(acc)
    quarter, column = iota_quarter(), iota_column()

    def step(r, _):
        lanes_a, lanes_o = ref_a[pl.ds(r, 1), :] & (LANES - 1), ref_o[pl.ds(r, 1), :] & (LANES - 1)
        w = jnp.broadcast_to(weight[pl.ds(r, 1), :], (8, LANES))
        values = [lead[pl.ds(r * 4, 8), :]]
        for at in (0, 8):
            a = gather_row(slabs[0], slots_a, r, TRACERS, at, lanes_a, quarter)
            o = gather_row(slabs[1], slots_o, r, TRACERS, at, lanes_o, quarter)
            values.append((a - o) * w)
        add_groups(scatter_row(values, lanes_a, lanes_o, column, quarter), slots_a, slots_o, r, *accs)
        return 0

    lax.fori_loop(0, nrows, step, 0, unroll=128)
    for n in range(9):
        p, q = n // 3, n % 3

        def split(c, _):
            for comp in range(2):
                at = pl.multiple_of((n * CAP + c) * 24, 8)
                to = pl.multiple_of(((p * 2 + comp) * CAP + c) * MIDDLE, 8)
                middle[q][pl.ds(to, MIDDLE), :] = accs[comp][pl.ds(at + 8, 8), :]
                to = ((q * 2 + comp) * CAP + c) * OUTER
                outer[p][pl.ds(to, 4), :] = accs[comp][pl.ds(at, 8), :][:4]
                outer[p][pl.ds(to + 4, 6), :] = accs[comp][pl.ds(at + 16, 8), :][:6]
            return 0

        lax.fori_loop(0, CAP, split, 0, unroll=8)


def scatter(slots, refs, weight, lead, pieces):
    nrows = weight.shape[0]
    return call(
        functools.partial(scatter_body, nrows),
        "scatter",
        (shape(3 * 2 * CAP * MIDDLE, LANES),) * 3 + (shape(3 * 2 * CAP * OUTER, LANES),) * 3,
        [SMEM] * 2 + [VMEM] * 9,
        [pltpu.VMEM((SLOTS * TRACERS + 8, LANES), F32)] * 2 + [pltpu.VMEM((SLOTS * 24, LANES), F32)] * 2,
        us=22,
    )(*slots, *refs, weight, lead, *pieces)


def add_middle_body(send_a, send_o, *rest):
    pieces, accs, (ids_a, ids_o, sems) = rest[:5], rest[5:7], rest[7:]
    copies = [pltpu.make_async_copy(s, to, sems.at[k]) for k, (s, to) in enumerate(((send_a, ids_a), (send_o, ids_o)))]
    for copy in copies:
        copy.start()
    for acc in accs:
        acc[...] = jnp.zeros_like(acc)
    for copy in copies:
        copy.wait()
    for n in range(9):

        def step(c, _):
            for comp, ids in enumerate((ids_a, ids_o)):
                at = pl.multiple_of(jnp.maximum(ids[n, 0, c], 0) * MIDDLE, 8)
                source, first = y_first_rows(pieces, n // 3, n % 3, comp, CAP)
                accs[comp][pl.ds(at, 8), :] += source[pl.ds(pl.multiple_of((first + c) * MIDDLE, 8), 8), :]
            return 0

        lax.fori_loop(0, CAP, step, 0, unroll=CAP)


def add_middle(send_a, send_o, nblocks, pieces):
    return call(
        add_middle_body,
        "add_middle",
        (shape(nblocks * MIDDLE, LANES),) * 2,
        [HBM] * 2 + [VMEM] * 5,
        [pltpu.SMEM(send_a.shape, jnp.int32)] * 2 + [pltpu.SemaphoreType.DMA((2,))],
        us=2,
    )(send_a, send_o, *pieces)


def unpack_body(nblocks, send_a, send_o, area_a, area_o, middle_a, middle_o, *rest):
    pieces, outs, accs, held, (ids_a, ids_o, sems, out_sems) = rest[:5], rest[5:7], rest[7:9], rest[9:11], rest[11:]
    copies = [pltpu.make_async_copy(s, to, sems.at[k]) for k, (s, to) in enumerate(((send_a, ids_a), (send_o, ids_o)))]
    for copy in copies:
        copy.start()
    for acc in accs:
        acc[...] = jnp.zeros_like(acc)
    for copy in copies:
        copy.wait()
    for n in range(9):

        def step(c, _):
            for comp, ids in enumerate((ids_a, ids_o)):
                at = pl.multiple_of(jnp.maximum(ids[n, 0, c], 0) * 16, 8)
                source, first = x_first_rows(pieces, n // 3, n % 3, comp, CAP)
                accs[comp][pl.ds(at, 8), :] += source[pl.ds((first + c) * OUTER, 8), :]
                accs[comp][pl.ds(at + 8, 2), :] += source[pl.ds((first + c) * OUTER + 8, 2), :]
            return 0

        lax.fori_loop(0, CAP, step, 0, unroll=CAP)
    quarters = 4
    size = nblocks // quarters
    leave = []
    for k in range(quarters):

        def finish(b, _):
            col = pl.ds(pl.multiple_of(b * LANES, LANES), LANES)
            for comp, (area, middle) in enumerate(((area_a, middle_a), (area_o, middle_o))):
                scale = 1.0 / area[pl.ds(b, 1), :]
                held[comp][0:4, col] = accs[comp][pl.ds(b * 16, 4), :] * scale
                held[comp][4:8, col] = middle[pl.ds(b * MIDDLE, 4), :] * scale
                held[comp][8:12, col] = middle[pl.ds(b * MIDDLE + 4, 4), :] * scale
                held[comp][12:16, col] = accs[comp][pl.ds(b * 16 + 4, 4), :] * scale
                held[comp][16:18, col] = accs[comp][pl.ds(b * 16 + 8, 2), :] * scale
            return 0

        lax.fori_loop(k * size, (k + 1) * size, finish, 0, unroll=8)
        here = pl.ds(k * size * LANES, size * LANES)
        for comp in range(2):
            copy = pltpu.make_async_copy(held[comp].at[:, here], outs[comp].at[:, here], out_sems.at[2 * k + comp])
            copy.start()
            leave.append(copy)
    for copy in leave:
        copy.wait()


def unpack(send_a, send_o, area_a, area_o, middle, outer):
    nblocks = area_a.shape[0]
    columns = nblocks * LANES
    return call(
        functools.partial(unpack_body, nblocks),
        "unpack",
        (shape(FLUXES, columns),) * 2,
        [HBM] * 2 + [VMEM] * 9,
        [pltpu.VMEM((nblocks * 16, LANES), F32)] * 2
        + [pltpu.VMEM((FLUXES, columns), F32)] * 2
        + [pltpu.SMEM(send_a.shape, jnp.int32)] * 2
        + [pltpu.SemaphoreType.DMA((2,)), pltpu.SemaphoreType.DMA((8,))],
        us=4,
        out_space=HBM,
    )(send_a, send_o, area_a, area_o, *add_middle(send_a, send_o, nblocks, middle), *outer)


def shards(fields_a, fields_o, area_a, area_o, send_a, send_o, atm_ref, ocn_ref, cell_area, cell_mask, cell_count):
    refs = (atm_ref.reshape(-1, LANES), ocn_ref.reshape(-1, LANES))
    send_a, send_o = send_a.transpose(1, 0, 2), send_o.transpose(1, 0, 2)
    lead_came, came = two_ways(*pack(send_a, send_o, fields_a, fields_o), 1)
    slots = group_slots(refs)
    weight, led = first(cell_count, slots, refs, cell_area.reshape(-1, LANES), cell_mask.reshape(-1, LANES), lead_came)
    sums = scatter(slots, refs, weight, led, came)
    middle, outer = two_ways(sums[:3], sums[3:], -1)
    return unpack(send_a, send_o, area_a.reshape(-1, LANES), area_o.reshape(-1, LANES), middle, outer)


def solution(mesh):
    both = ("gx", "gy")
    in_specs = (P(None, both), P(None, both), P(both), P(both), P(both, None, None), P(both, None, None)) + (P(both),) * 5
    return jax.shard_map(shards, mesh=mesh, in_specs=in_specs, out_specs=(P(None, both),) * 2, check_vma=False)
```

```python
import functools

import jax
import jax.numpy as jnp
import numpy as np
from jax import lax
from jax.experimental import pallas as pl
from jax.experimental.pallas import tpu as pltpu
from jax.sharding import PartitionSpec as P

ITERS = 6
GRP = 32
LANES = 128
CAP = 24
SLOTS = 9 * CAP
LEAD = 6
TRACERS = 14
FLUXES = 18
MIDDLE = 8
OUTER = 10

HBM = pl.BlockSpec(memory_space=pltpu.HBM)
VMEM = pl.BlockSpec(memory_space=pltpu.VMEM)
SMEM = pl.BlockSpec(memory_space=pltpu.SMEM)
F32 = jnp.float32
BF16 = jnp.bfloat16


def cost(us):
    return pl.CostEstimate(flops=0, bytes_accessed=int(us * 3.3e6), transcendentals=0)


def call(body, name, out_shape, in_specs, scratch=(), us=10, limit=40, out_space=VMEM):
    return pl.pallas_call(
        body,
        name=name,
        out_shape=out_shape,
        in_specs=in_specs,
        out_specs=jax.tree.map(lambda _: out_space, out_shape),
        scratch_shapes=list(scratch),
        compiler_params=pltpu.CompilerParams(vmem_limit_bytes=limit * 1024 * 1024),
        cost_estimate=cost(us),
    )


def shape(*dims):
    return jax.ShapeDtypeStruct(dims, F32)


def block_column(ids, n, c):
    return pl.ds(pl.multiple_of(jnp.maximum(ids[n, 0, c], 0) * LANES, LANES), LANES)


def pack_body(send_a, send_o, fields_a, fields_o, *rest):
    outs, (ids_a, ids_o, top_a, top_o, low_a, low_o), held, in_sems, out_sems = (
        rest[:6],
        rest[6:12],
        rest[12:18],
        rest[18],
        rest[19],
    )
    lead, tracers = held[:3], held[3:]
    count = fields_a.shape[0]
    moves = [(send_a, ids_a), (send_o, ids_o)]
    moves += [(f.at[pl.ds(0, 8), :], to) for f, to in ((fields_a, top_a), (fields_o, top_o))]
    moves += [(f.at[pl.ds(8, count - 8), :], to) for f, to in ((fields_a, low_a), (fields_o, low_o))]
    copies = [pltpu.make_async_copy(source, to, in_sems.at[k]) for k, (source, to) in enumerate(moves)]
    leave = [pltpu.make_async_copy(source, to, out_sems.at[k]) for k, (source, to) in enumerate(zip(held, outs))]
    for copy in copies:
        copy.start()
    for copy in copies[:4]:
        copy.wait()
    sides = ((ids_a, top_a, low_a), (ids_o, top_o, low_o))
    for n in range(9):
        p, q = n // 3, n % 3

        def lead_step(c, _):
            for comp, (ids, top, _) in enumerate(sides):
                v = top[:, block_column(ids, n, c)]
                lead[q][pl.ds(((p * 2 + comp) * CAP + c) * LEAD, LEAD), :] = v[:LEAD]
                tracers[p][pl.ds(((q * 2 + comp) * CAP + c) * TRACERS, 2), :] = v[LEAD:]
            return 0

        lax.fori_loop(0, CAP, lead_step, 0, unroll=CAP)
    for copy in leave[:3]:
        copy.start()
    for copy in copies[4:]:
        copy.wait()
    for n in range(9):
        p, q = n // 3, n % 3

        def step(c, _):
            for comp, (ids, _, low) in enumerate(sides):
                col = block_column(ids, n, c)
                row = ((q * 2 + comp) * CAP + c) * TRACERS + 2
                tracers[p][pl.ds(row, 8), :] = low[0:8, col]
                tracers[p][pl.ds(row + 8, 4), :] = low[8:12, col]
            return 0

        lax.fori_loop(0, CAP, step, 0, unroll=CAP)
        if q == 2:
            leave[3 + p].start()
    for copy in leave:
        copy.wait()


def pack(send_a, send_o, fields_a, fields_o):
    count, columns = fields_a.shape
    outs = (shape(3 * 2 * CAP * LEAD, LANES),) * 3 + (shape(3 * 2 * CAP * TRACERS, LANES),) * 3
    outs = call(
        pack_body,
        "pack",
        outs,
        [HBM] * 4,
        [pltpu.SMEM(send_a.shape, jnp.int32)] * 2
        + [pltpu.VMEM((8, columns), F32)] * 2
        + [pltpu.VMEM((count - 8, columns), F32)] * 2
        + [pltpu.VMEM(o.shape, F32) for o in outs]
        + [pltpu.SemaphoreType.DMA((6,))] * 2,
        us=4,
        limit=63,
        out_space=HBM,
    )(send_a, send_o, fields_a, fields_o)
    return outs[:3], outs[3:]


def hop(value, axis, steps):
    count = lax.axis_size(axis)
    return lax.ppermute(value, axis, [(s, (s + steps) % count) for s in range(count)])


def third(value, k):
    size = value.shape[0] // 3
    return value[k * size : (k + 1) * size]


def two_ways(y_first, x_first, sign):
    y = [hop(y_first[0], "gy", -sign), y_first[1], hop(y_first[2], "gy", sign)]
    x = [hop(x_first[0], "gx", -sign), x_first[1], hop(x_first[2], "gx", sign)]
    sides = [jnp.concatenate([third(v, k) for v in x]) for k in (0, 2)]
    *_, y[0], y[2] = lax.optimization_barrier((*sides, y[0], y[2]))
    ends = [jnp.concatenate([third(v, k) for v in y]) for k in (0, 2)]
    behind, ahead = hop(ends[0], "gx", -sign), hop(ends[1], "gx", sign)
    down, up = hop(sides[0], "gy", -sign), hop(sides[1], "gy", sign)
    return (behind, ahead, *y), (down, up, *x)


def y_first_rows(pieces, p, q, comp, size):
    behind, ahead, *came = pieces
    if p == 1:
        return came[q], (2 + comp) * size
    return (behind, None, ahead)[p], (q * 2 + comp) * size


def x_first_rows(pieces, p, q, comp, size):
    down, up, *came = pieces
    if q == 1:
        return came[p], (2 + comp) * size
    return (down, None, up)[q], (p * 2 + comp) * size


def join_slabs(find, pieces, slabs, rows):
    for n in range(9):
        for comp in range(2):
            source, at = find(pieces, n // 3, n % 3, comp, rows)
            slabs[comp][pl.ds(n * rows, rows), :] = source[pl.ds(at, rows), :]


def take_lanes(v, index):
    dims = lax.GatherDimensionNumbers(
        offset_dims=(),
        collapsed_slice_dims=(1,),
        start_index_map=(1,),
        operand_batching_dims=(0,),
        start_indices_batching_dims=(0,),
    )
    return lax.gather(v, index[..., None], dims, (1, 1), mode=lax.GatherScatterMode.PROMISE_IN_BOUNDS)


def gather_row(slab, slots, r, stride, first, lanes, quarter):
    out = None
    index = jnp.broadcast_to(lanes, (8, LANES))
    for j in range(4):
        v = take_lanes(slab[pl.ds(slots[j, r] * stride + first, 8), :], index)
        out = v if out is None else jnp.where(quarter >= j, v, out)
    return out


def odd_arctan_coefficients():
    z_top = 0.325
    nodes = (np.cos((np.arange(400) + 0.5) * np.pi / 400) + 1) / 2 * z_top
    t = np.sqrt(nodes)
    fit = np.polynomial.chebyshev.Chebyshev.fit(nodes, np.arctan(t) / t, 7, domain=[0, z_top])
    return [float(c) for c in fit.convert(kind=np.polynomial.Polynomial).coef]


ARCTAN = odd_arctan_coefficients()


def small_arctan(t):
    z = t * t
    total = jnp.full_like(t, ARCTAN[-1])
    for c in ARCTAN[-2::-1]:
        total = total * z + c
    return t * total


def bulk(a, o):
    shear_x = 6.0 * a[0] - 0.3 * o[0]
    shear_y = 6.0 * a[1] - 0.3 * o[1]
    speed2 = shear_x * shear_x + shear_y * shear_y + 0.25 + 0.1 * a[5] * a[5]
    speed = jnp.sqrt(speed2)
    dtemp = 3.0 * (a[2] - o[2])
    dhum = 0.002 * (a[3] - o[3])
    height = 10.0 * jnp.exp(0.3 * a[4])
    log_height = jnp.log(height * 10000.0)
    log_m = log_height - 0.5 * o[4]
    log_h = log_height - 0.5 * o[5]
    rm = 0.4 / log_m
    rh = 0.4 / log_h
    base = (0.4 * 9.8) * height * (dtemp / 290.0 + 0.61 * dhum) / speed2
    for _ in range(ITERS):
        zeta = jnp.clip(base * rh / (rm * rm), -10.0, 3.0)
        u2 = jnp.sqrt(1.0 - 16.0 * jnp.minimum(zeta, 0.0))
        u = jnp.sqrt(u2)
        one_u = 1.0 + u
        one_u2 = 1.0 + u2
        stable = -5.0 * zeta
        psi_m = jnp.where(
            zeta > 0.0,
            stable,
            jnp.log(one_u * one_u * one_u2 * 0.125) - 2.0 * small_arctan((u - 1.0) / one_u),
        )
        psi_h = jnp.where(zeta > 0.0, stable, 2.0 * jnp.log(one_u2 * 0.5))
        rm = 0.5 * rm + 0.2 / (log_m - psi_m)
        rh = 0.5 * rh + 0.2 / (log_h - psi_h)
    drag = 25.0 * rm * rm * speed
    transfer = 25.0 * rm * rh * speed
    return (drag * shear_x, drag * shear_y, transfer * dtemp, 500.0 * transfer * dhum), transfer


def onehots(lanes_a, lanes_o, column):
    one, zero = jnp.ones((), BF16), jnp.zeros((), BF16)
    a = jnp.where(column == lanes_a.astype(BF16), one, zero)
    o = jnp.where(column == lanes_o.astype(BF16), one, zero)
    return jnp.concatenate([a, o], axis=0)


def two_pieces(v):
    high = v.astype(BF16).astype(F32)
    return high, v - high


def scatter_row(values, lanes_a, lanes_o, column, quarter):
    def masked(v):
        return [jnp.where(quarter == j, v, 0.0) for j in range(4)]

    halves = []
    for pieces in zip(*(two_pieces(v) for v in values)):
        lead, one, two = map(masked, pieces)
        halves.append(jnp.concatenate([x for pair in zip(one, two) for x in pair] + lead, axis=0).astype(BF16))
    left = jnp.concatenate(halves, axis=1)
    right = onehots(lanes_a, lanes_o, column)
    right = jnp.concatenate([right, right], axis=1)
    sums = lax.dot_general(left, right, (((1,), (1,)), ((), ())), preferred_element_type=F32)
    return [[sums[at : at + 8] for at in (64 + 8 * j, 16 * j, 16 * j + 8)] for j in range(4)]


def add_groups(sums, slots_a, slots_o, r, acc_a, acc_o):
    for j in range(4):
        base_a, base_o = slots_a[j, r] * 24, slots_o[j, r] * 24
        for k, x in enumerate(sums[j]):
            acc_a[pl.ds(pl.multiple_of(base_a + 8 * k, 8), 8), :] += x[:, :LANES]
            acc_o[pl.ds(pl.multiple_of(base_o + 8 * k, 8), 8), :] += x[:, LANES:]


def slots_body(ref_a, ref_o, out_a, out_o):
    pick = jnp.where(
        lax.broadcasted_iota(jnp.int32, (8, LANES), 1) == GRP * lax.broadcasted_iota(jnp.int32, (8, LANES), 0), 1.0, 0.0
    ).astype(BF16)
    for ref, out in ((ref_a, out_a), (ref_o, out_o)):
        slot = (ref[...] >> 7).astype(F32).astype(BF16)
        picked = lax.dot_general(pick, slot, (((1,), (1,)), ((), ())), preferred_element_type=F32)
        out[...] = picked.astype(jnp.int32)


def group_slots(refs):
    out = (jax.ShapeDtypeStruct((8, refs[0].shape[0]), jnp.int32),) * 2
    return call(slots_body, "slots", out, [VMEM, VMEM], us=1)(*refs)


def iota_quarter():
    return lax.broadcasted_iota(jnp.int32, (8, LANES), 1) // GRP


def iota_column():
    return lax.broadcasted_iota(jnp.int32, (LANES, LANES), 0).astype(BF16)


def first_body(nrows, count, slots_a, slots_o, ref_a, ref_o, area, mask, *rest):
    pieces, (weight, lead, slab_a, slab_o, cells_a, cells_o) = rest[:5], rest[5:]
    join_slabs(y_first_rows, pieces, (slab_a, slab_o), CAP * LEAD)
    quarter = iota_quarter()

    def gather(r, _):
        for ref, slab, slots, cells in ((ref_a, slab_a, slots_a, cells_a), (ref_o, slab_o, slots_o, cells_o)):
            lanes = ref[pl.ds(r, 1), :] & (LANES - 1)
            cells[pl.ds(r, 8, stride=nrows), :] = gather_row(slab, slots, r, LEAD, 0, lanes, quarter)
        return 0

    lax.fori_loop(0, nrows, gather, 0, unroll=128)
    live = count[0]
    depth = 64

    def iterate(i, _):
        row = pl.multiple_of(i * depth, depth)
        a = [cells_a[pl.ds(pl.multiple_of(f * nrows + row, depth), depth), :] for f in range(6)]
        o = [cells_o[pl.ds(pl.multiple_of(f * nrows + row, depth), depth), :] for f in range(6)]
        here = pl.ds(row, depth)
        place = (row + lax.broadcasted_iota(jnp.int32, (depth, LANES), 0)) * LANES
        place = place + lax.broadcasted_iota(jnp.int32, (depth, LANES), 1)
        w = jnp.where((place < live) & (mask[here, :] == 1), area[here, :], 0.0)
        fluxes, transfer = bulk(a, o)
        weight[here, :] = transfer * w
        for k, flux in enumerate(fluxes):
            lead[pl.ds(row * 4 + k, depth, stride=4), :] = flux * w
        return 0

    lax.fori_loop(0, nrows // depth, iterate, 0)


def first(count, slots, refs, area, mask, pieces):
    nrows = area.shape[0]
    return call(
        functools.partial(first_body, nrows),
        "bulk",
        (shape(nrows, LANES), shape(nrows * 4 + 8, LANES)),
        [SMEM] * 3 + [VMEM] * 9,
        [pltpu.VMEM((SLOTS * LEAD + 8, LANES), F32)] * 2 + [pltpu.VMEM((8 * nrows, LANES), F32)] * 2,
        us=20,
    )(count, *slots, *refs, area, mask, *pieces)


def scatter_body(nrows, slots_a, slots_o, ref_a, ref_o, weight, lead, *rest):
    pieces, middle, outer, slabs, accs = rest[:5], rest[5:8], rest[8:11], rest[11:13], rest[13:]
    join_slabs(x_first_rows, pieces, slabs, CAP * TRACERS)
    for acc in accs:
        acc[...] = jnp.zeros_like(acc)
    quarter, column = iota_quarter(), iota_column()

    def step(r, _):
        lanes_a, lanes_o = ref_a[pl.ds(r, 1), :] & (LANES - 1), ref_o[pl.ds(r, 1), :] & (LANES - 1)
        w = jnp.broadcast_to(weight[pl.ds(r, 1), :], (8, LANES))
        values = [lead[pl.ds(r * 4, 8), :]]
        for at in (0, 8):
            a = gather_row(slabs[0], slots_a, r, TRACERS, at, lanes_a, quarter)
            o = gather_row(slabs[1], slots_o, r, TRACERS, at, lanes_o, quarter)
            values.append((a - o) * w)
        add_groups(scatter_row(values, lanes_a, lanes_o, column, quarter), slots_a, slots_o, r, *accs)
        return 0

    lax.fori_loop(0, nrows, step, 0, unroll=256)
    for n in range(9):
        p, q = n // 3, n % 3

        def split(c, _):
            for comp in range(2):
                at = pl.multiple_of((n * CAP + c) * 24, 8)
                to = pl.multiple_of(((p * 2 + comp) * CAP + c) * MIDDLE, 8)
                middle[q][pl.ds(to, MIDDLE), :] = accs[comp][pl.ds(at + 8, 8), :]
                to = ((q * 2 + comp) * CAP + c) * OUTER
                outer[p][pl.ds(to, 4), :] = accs[comp][pl.ds(at, 8), :][:4]
                outer[p][pl.ds(to + 4, 6), :] = accs[comp][pl.ds(at + 16, 8), :][:6]
            return 0

        lax.fori_loop(0, CAP, split, 0, unroll=CAP)


def scatter(slots, refs, weight, lead, pieces):
    nrows = weight.shape[0]
    return call(
        functools.partial(scatter_body, nrows),
        "scatter",
        (shape(3 * 2 * CAP * MIDDLE, LANES),) * 3 + (shape(3 * 2 * CAP * OUTER, LANES),) * 3,
        [SMEM] * 2 + [VMEM] * 9,
        [pltpu.VMEM((SLOTS * TRACERS + 8, LANES), F32)] * 2 + [pltpu.VMEM((SLOTS * 24, LANES), F32)] * 2,
        us=22,
    )(*slots, *refs, weight, lead, *pieces)


def add_middle_body(send_a, send_o, *rest):
    pieces, accs, (ids_a, ids_o, sems) = rest[:5], rest[5:7], rest[7:]
    copies = [pltpu.make_async_copy(s, to, sems.at[k]) for k, (s, to) in enumerate(((send_a, ids_a), (send_o, ids_o)))]
    for copy in copies:
        copy.start()
    for acc in accs:
        acc[...] = jnp.zeros_like(acc)
    for copy in copies:
        copy.wait()
    for n in range(9):

        def step(c, _):
            for comp, ids in enumerate((ids_a, ids_o)):
                at = pl.multiple_of(jnp.maximum(ids[n, 0, c], 0) * MIDDLE, 8)
                source, first = y_first_rows(pieces, n // 3, n % 3, comp, CAP)
                accs[comp][pl.ds(at, 8), :] += source[pl.ds(pl.multiple_of((first + c) * MIDDLE, 8), 8), :]
            return 0

        lax.fori_loop(0, CAP, step, 0, unroll=CAP)


def add_middle(send_a, send_o, nblocks, pieces):
    return call(
        add_middle_body,
        "add_middle",
        (shape(nblocks * MIDDLE, LANES),) * 2,
        [HBM] * 2 + [VMEM] * 5,
        [pltpu.SMEM(send_a.shape, jnp.int32)] * 2 + [pltpu.SemaphoreType.DMA((2,))],
        us=2,
    )(send_a, send_o, *pieces)


def unpack_body(nblocks, send_a, send_o, area_a, area_o, middle_a, middle_o, *rest):
    pieces, outs, accs, held, (ids_a, ids_o, sems, out_sems) = rest[:5], rest[5:7], rest[7:9], rest[9:11], rest[11:]
    copies = [pltpu.make_async_copy(s, to, sems.at[k]) for k, (s, to) in enumerate(((send_a, ids_a), (send_o, ids_o)))]
    for copy in copies:
        copy.start()
    for acc in accs:
        acc[...] = jnp.zeros_like(acc)
    for copy in copies:
        copy.wait()
    for n in range(9):

        def step(c, _):
            for comp, ids in enumerate((ids_a, ids_o)):
                at = pl.multiple_of(jnp.maximum(ids[n, 0, c], 0) * 16, 8)
                source, first = x_first_rows(pieces, n // 3, n % 3, comp, CAP)
                accs[comp][pl.ds(at, 8), :] += source[pl.ds((first + c) * OUTER, 8), :]
                accs[comp][pl.ds(at + 8, 2), :] += source[pl.ds((first + c) * OUTER + 8, 2), :]
            return 0

        lax.fori_loop(0, CAP, step, 0, unroll=CAP)
    quarters = 4
    size = nblocks // quarters
    leave = []
    for k in range(quarters):

        def finish(b, _):
            col = pl.ds(pl.multiple_of(b * LANES, LANES), LANES)
            for comp, (area, middle) in enumerate(((area_a, middle_a), (area_o, middle_o))):
                scale = 1.0 / area[pl.ds(b, 1), :]
                held[comp][0:4, col] = accs[comp][pl.ds(b * 16, 4), :] * scale
                held[comp][4:8, col] = middle[pl.ds(b * MIDDLE, 4), :] * scale
                held[comp][8:12, col] = middle[pl.ds(b * MIDDLE + 4, 4), :] * scale
                held[comp][12:16, col] = accs[comp][pl.ds(b * 16 + 4, 4), :] * scale
                held[comp][16:18, col] = accs[comp][pl.ds(b * 16 + 8, 2), :] * scale
            return 0

        lax.fori_loop(k * size, (k + 1) * size, finish, 0, unroll=8)
        here = pl.ds(k * size * LANES, size * LANES)
        for comp in range(2):
            copy = pltpu.make_async_copy(held[comp].at[:, here], outs[comp].at[:, here], out_sems.at[2 * k + comp])
            copy.start()
            leave.append(copy)
    for copy in leave:
        copy.wait()


def unpack(send_a, send_o, area_a, area_o, middle, outer):
    nblocks = area_a.shape[0]
    columns = nblocks * LANES
    return call(
        functools.partial(unpack_body, nblocks),
        "unpack",
        (shape(FLUXES, columns),) * 2,
        [HBM] * 2 + [VMEM] * 9,
        [pltpu.VMEM((nblocks * 16, LANES), F32)] * 2
        + [pltpu.VMEM((FLUXES, columns), F32)] * 2
        + [pltpu.SMEM(send_a.shape, jnp.int32)] * 2
        + [pltpu.SemaphoreType.DMA((2,)), pltpu.SemaphoreType.DMA((8,))],
        us=4,
        out_space=HBM,
    )(send_a, send_o, area_a, area_o, *add_middle(send_a, send_o, nblocks, middle), *outer)


def shards(fields_a, fields_o, area_a, area_o, send_a, send_o, atm_ref, ocn_ref, cell_area, cell_mask, cell_count):
    refs = (atm_ref.reshape(-1, LANES), ocn_ref.reshape(-1, LANES))
    send_a, send_o = send_a.transpose(1, 0, 2), send_o.transpose(1, 0, 2)
    lead_came, came = two_ways(*pack(send_a, send_o, fields_a, fields_o), 1)
    slots = group_slots(refs)
    weight, led = first(cell_count, slots, refs, cell_area.reshape(-1, LANES), cell_mask.reshape(-1, LANES), lead_came)
    sums = scatter(slots, refs, weight, led, came)
    middle, outer = two_ways(sums[:3], sums[3:], -1)
    return unpack(send_a, send_o, area_a.reshape(-1, LANES), area_o.reshape(-1, LANES), middle, outer)


def solution(mesh):
    both = ("gx", "gy")
    in_specs = (P(None, both), P(None, both), P(both), P(both), P(both, None, None), P(both, None, None)) + (P(both),) * 5
    return jax.shard_map(shards, mesh=mesh, in_specs=in_specs, out_specs=(P(None, both),) * 2, check_vma=False)
```
